256 devices in a mesh: dp: 32 (over z, y), tp: 8 (over x, core).
Axes of the slice: x: 4, y: 4, z: 8, core: 2. Of those that a mesh axis runs over, the one named last changes fastest.
Arguments:
- prefill_latent: bfloat16 [16384, 576], P('dp'), may hold values from -5 to 5
- request_slot: int32 [128], replicated, may hold values from 0 to 127, each once
- new_lengths: int32 [32, 4], replicated, may hold values from 1 to 8, 16 in all within a row
- ctx_lengths: int32 [128], P('dp'), may hold values from 1 to 1024, 65536 in all
- kv_cache: bfloat16 [128, 1024, 576], P('dp'), may hold values from -5 to 5
- queries: bfloat16 [2, 128, 128, 576], P(None, 'dp', 'tp'), may hold values from -48 to 48
- step_latents: bfloat16 [2, 128, 576], P(None, 'dp'), may hold values from -5 to 5
- w_uv: bfloat16 [128, 512, 128], P('tp'), may hold values from -0.25 to 0.25
- w_out: bfloat16 [128, 128, 7168], P('tp', None, 'dp'), may hold values from -0.09375 to 0.09375
- hidden: bfloat16 [2, 128, 7168], P(None, None, ('dp', 'tp')), may hold values from -2 to 2
- ffn_gain: float32 [7168], replicated, may hold values from 0.5 to 1.5
- w_gate: bfloat16 [7168, 18432], P(None, ('dp', 'tp')), may hold values from -0.0625 to 0.0625
- w_up: bfloat16 [7168, 18432], P(None, ('dp', 'tp')), may hold values from -0.0625 to 0.0625
- w_down: bfloat16 [18432, 7168], P(('dp', 'tp')), may hold values from -0.1875 to 0.1875
Outputs:
- layer_out: bfloat16 [2, 128, 7168], P(None, None, ('dp', 'tp'))
The draws below stay inside these ranges and needn't reach their ends.
Inputs may be any that keep to these rules, and one draw needn't show every extreme that they name: A permutation of the 128 requests; the owner of request r is request_slot[r] // 4. `new_lengths`: row j lists the 4 requests of owner j; each row sums to 16, and its largest entry is 8. `ctx_lengths`: sums to 65536; the largest is 1024.
All inputs are finite; a program needn't handle non-finite values. No bound on the sum of `ctx_lengths` on one device may be relied on, other than what follows from the above.
Results may differ from the reference program's by a relative error of at most 0.02.
Values may be sent and summed in bfloat16 or wider, within the bound.
No kernel may reach another device: no remote copies, remote signals or barrier semaphores. Data moves between devices by JAX's collectives and lax.ppermute only.
A program may use at most 128 MiB of HBM per device.

```python
import math
import jax
import jax.numpy as jnp
import numpy as np
from jax import lax

D = 7168
H = 128
LAT = 512
ROPE = 64
VH = 128
QKD = 192
FF = 18432
RQ = 4
OWN_TOK = 16
CTX_MOST = 1024
STEPS = 2
R = 128
PF_DEV = 512
SEG_MOST = 8
CTX_TOTAL = 65536
N_DP = 32


def latent_pair(key):
    base = jnp.clip(jax.random.normal(jax.random.fold_in(key, 101), (R, CTX_MOST, LAT + ROPE), jnp.float32), -5.0, 5.0)
    return base


def draw_kv_cache(key, part):
    base = latent_pair(key)
    return base.astype(jnp.bfloat16)


def draw_queries(key, part):
    key = jax.random.fold_in(key, 5)
    values = jnp.clip(jax.random.normal(key, (STEPS, R, H, LAT + ROPE), jnp.float32), -5.0, 5.0)
    return values.astype(jnp.bfloat16)


def strengthened(values, rng, source, target, parts, factor):
    def block_of(dim):
        return (jnp.arange(values.shape[dim]) // (values.shape[dim] // parts)).reshape((-1,) + (1,) * (values.ndim - 1 - dim))

    first = jax.random.permutation(rng, parts)[block_of(target)]
    far = (block_of(target) + parts // 2) % parts
    return jnp.where((block_of(source) == first) | (block_of(source) == far), factor * values, values)


def block_levels(stream_key, extent, pieces, smallest, largest):
    factor_of, own = 1.0, jax.random.fold_in(stream_key, 6)
    for dim, blocks in pieces:
        steps = jnp.exp(jax.random.uniform(jax.random.fold_in(own, dim), (blocks,), jnp.float32, smallest / len(pieces), largest / len(pieces)))
        factor_of = factor_of * jnp.repeat(steps, extent[dim] // blocks).reshape([-1 if axis == dim else 1 for axis in range(len(extent))])
    return factor_of


def profile(count, total, reach, skew):
    portions = [(1 << 20) // math.isqrt(standing ** skew) + 1 for standing in range(2, count + 1)]
    rest, holding = total - reach - (count - 1), [1] * (count - 1)
    while rest > 0:
        movable = [i for i in range(count - 1) if holding[i] < reach]
        pool, budget = sum([portions[i] for i in movable]), rest
        for i in movable:
            extra = min(reach - holding[i], max(1, budget * portions[i] // pool), rest)
            holding[i] = holding[i] + extra
            rest = rest - extra
    return np.array([reach] + holding)


def uneven_parts(rng, number_of, total, most, slope):
    if number_of == 2:
        one = jax.random.randint(rng, (), max(1, total - most), min(most, total - 1) + 1)
        return jnp.stack([one, total - one])
    tallies = jnp.asarray(profile(number_of, total, most, slope), jnp.int32)
    couples = (number_of - 1) // 2
    source_of, sink = tallies[1:1 + 2 * couples:2], tallies[2:2 + 2 * couples:2]
    room = jnp.minimum(source_of - 1, most - sink)
    moved = jax.random.randint(jax.random.fold_in(rng, 1), (couples,), 0, 1 << 20) % (room + 1)
    tallies = tallies.at[1:1 + 2 * couples:2].set(source_of - moved).at[2:2 + 2 * couples:2].set(sink + moved)
    return tallies[jax.random.permutation(jax.random.fold_in(rng, 2), number_of)]


def scatter_about(own_key, extent, deviation, limit, split=(), kind=jnp.bfloat16):
    values = deviation * jax.random.normal(own_key, extent, jnp.float32)
    if split:
        values = values * block_levels(own_key, extent, split, -0.22, 0.18)
    return jnp.clip(values, -limit, limit).astype(kind)


def bell_draw_with(key, extent, scale, bound, split, heavy, kind=jnp.bfloat16):
    entries = scale * jax.random.normal(key, extent, jnp.float32)
    if split:
        entries = entries * block_levels(key, extent, split, -0.22, 0.18)
    return jnp.clip(strengthened(entries, jax.random.fold_in(key, 3), *heavy), -bound, bound).astype(kind)


def setup_inputs(seed: int = 0) -> dict:
    seeds = jax.random.split(jax.random.key(seed), 15)
    return {
        "prefill_latent": scatter_about(seeds[0], (N_DP * PF_DEV, LAT + ROPE), 1.0, 5.0, ((0, 32),)),
        "request_slot": jax.random.permutation(seeds[1], R).astype(jnp.int32),
        "new_lengths": jax.vmap(lambda own: uneven_parts(own, RQ, OWN_TOK, OWN_TOK // 2, 1))(jax.random.split(seeds[2], N_DP)).reshape((N_DP, RQ)).astype(jnp.int32),
        "ctx_lengths": uneven_parts(seeds[3], R, CTX_TOTAL, CTX_MOST, 2).astype(jnp.int32),
        "kv_cache": draw_kv_cache(jax.random.fold_in(seeds[14], 71), 0),
        "queries": draw_queries(jax.random.fold_in(seeds[14], 71), 0),
        "step_latents": scatter_about(seeds[6], (STEPS, R, LAT + ROPE), 1.0, 5.0, ((1, 32),)),
        "w_uv": scatter_about(seeds[7], (H, LAT, VH), LAT ** -0.5, 0.25, ((0, 8),)),
        "w_out": bell_draw_with(seeds[8], (H, VH, D), (H * VH) ** -0.5, 0.09375, ((0, 8), (2, 32)), (0, 2, 32, 2.75)),
        "hidden": scatter_about(seeds[9], (STEPS, R, D), 0.3, 2.0, ((2, 256),)),
        "ffn_gain": jnp.clip(1.0 + 0.1 * jax.random.normal(seeds[10], (D,), jnp.float32), 0.5, 1.5),
        "w_gate": scatter_about(seeds[11], (D, FF), D ** -0.5, 0.0625, ((1, 256),)),
        "w_up": scatter_about(seeds[12], (D, FF), D ** -0.5, 0.0625, ((1, 256),)),
        "w_down": bell_draw_with(seeds[13], (FF, D), FF ** -0.5, 0.1875, ((0, 256),), (0, 1, 256, 6.0)),
    }


masked_score = -1e+30
norm_eps = 1e-06

def reference(prefill_latent, request_slot, new_lengths, ctx_lengths, kv_cache, queries, step_latents, w_uv, w_out, hidden, ffn_gain, w_gate, w_up, w_down):
    score_scale = QKD ** (-0.5)
    lengths_flat = new_lengths.reshape(-1)
    request_rows = lengths_flat[request_slot]
    offsets = (jnp.cumsum(request_rows) - request_rows).astype(jnp.int32)
    inverse = jnp.zeros((R,), jnp.int32).at[request_slot].set(jnp.arange(R, dtype=jnp.int32))
    span = jnp.arange(SEG_MOST, dtype=jnp.int32)
    outputs = []
    for step in range(STEPS):

        def attend_one(q_index):
            request = inverse[q_index]
            count = lengths_flat[q_index]
            key_rows = (jnp.arange(N_DP, dtype=jnp.int32)[:, None] * PF_DEV + offsets[request] + span[None, :]).reshape(-1)
            key_rows = jnp.minimum(key_rows, N_DP * PF_DEV - 1).astype(jnp.int32)
            new_keys = prefill_latent[key_rows]
            new_valid = jnp.tile(span < count, N_DP)
            cache_valid = jnp.arange(CTX_MOST, dtype=jnp.int32) < ctx_lengths[q_index]
            all_keys = jnp.concatenate([kv_cache[q_index], new_keys, step_latents[:step + 1, q_index]], axis=0).astype(jnp.float32)
            valid = jnp.concatenate([cache_valid, new_valid, jnp.ones((step + 1,), bool)])
            query = queries[step, q_index].astype(jnp.float32)
            scores = jnp.dot(query, all_keys.T, precision=lax.Precision.HIGHEST, preferred_element_type=jnp.float32) * score_scale
            scores = jnp.where(valid[None, :], scores, masked_score)
            probs = jax.nn.softmax(scores, axis=-1).astype(jnp.bfloat16)
            latent_out = jnp.dot(probs.astype(jnp.float32), all_keys[:, :LAT], precision=lax.Precision.HIGHEST, preferred_element_type=jnp.float32)
            return latent_out.astype(jnp.bfloat16)
        latent_all = lax.map(attend_one, jnp.arange(R, dtype=jnp.int32))
        head_out = jnp.einsum('rhc,hcv->rhv', latent_all.astype(jnp.float32), w_uv.astype(jnp.float32), precision=lax.Precision.HIGHEST).astype(jnp.bfloat16)
        mixed = hidden[step].astype(jnp.float32) + jnp.dot(head_out.reshape(R, H * VH), w_out.reshape(H * VH, D), preferred_element_type=jnp.float32)
        mean_square = lax.optimization_barrier(jnp.mean(mixed * mixed, axis=-1, keepdims=True))
        normed = (mixed * lax.rsqrt(mean_square + norm_eps) * ffn_gain).astype(jnp.bfloat16)
        gate_out = jnp.dot(normed, w_gate, preferred_element_type=jnp.float32)
        up_out = jnp.dot(normed, w_up, preferred_element_type=jnp.float32)
        activated = (jax.nn.silu(gate_out) * up_out).astype(jnp.bfloat16)
        layer_step = mixed + jnp.dot(activated, w_down, preferred_element_type=jnp.float32)
        outputs.append(layer_step.astype(jnp.bfloat16))
    return jnp.stack(outputs, axis=0)
```

```python
import functools

import jax
import jax.numpy as jnp
from jax import lax
from jax.experimental import pallas as pl
from jax.experimental.pallas import tpu as pltpu
from jax.sharding import PartitionSpec as P

LAT = 512
QKD = 192
OWN_TOK = 16
PAD = 32
GROUP = 4

masked_score = -1e30
norm_eps = 1e-06
bf16, f32, i32 = jnp.bfloat16, jnp.float32, jnp.int32

NT = (((1,), (1,)), ((), ()))
NN = (((1,), (0,)), ((), ()))


def dot(a, b, dims=NN):
    return lax.dot_general(a, b, dims, preferred_element_type=f32)


def iota(shape, dim):
    return lax.broadcasted_iota(i32, shape, dim)


def call(body, out_shape, cost=(0, 0), **kwargs):
    return pl.pallas_call(
        body,
        out_shape=out_shape,
        compiler_params=pltpu.CompilerParams(vmem_limit_bytes=40 * 1024 * 1024),
        cost_estimate=pl.CostEstimate(flops=cost[0], bytes_accessed=cost[1], transcendentals=0),
        **kwargs,
    )


def share_picker(tp, width):
    shape = (tp * PAD, tp * width)
    row = iota(shape, 0)
    place = row % PAD
    wanted = (row // PAD) * width + place
    return jnp.where((iota(shape, 1) == wanted) & (place < width), 1.0, 0.0).astype(bf16)


def token_picker(dp, per_owner, steps):
    total = dp * per_owner * steps
    shape = (total, total)
    row = iota(shape, 0)
    step, request = row // (dp * per_owner), row % (dp * per_owner)
    wanted = request * steps + step
    return jnp.where(iota(shape, 1) == wanted, 1.0, 0.0).astype(bf16)


def route_kernel(slot_col, slot_row, len_col, len_row, rows_ref, out_ref):
    count = slot_col.shape[0]
    total = rows_ref.shape[0]
    square = (count, count)
    sub, lane = iota(square, 0), iota(square, 1)
    hot = slot_col[...] == lane
    hot_t = sub == slot_row[...]
    rows_col = jnp.sum(jnp.where(hot, len_row[...], 0), axis=1, keepdims=True)
    rows_row = jnp.sum(jnp.where(hot_t, len_col[...], 0), axis=0, keepdims=True)
    owner_start = jnp.sum(jnp.where(sub < lane, len_col[...], 0), axis=0, keepdims=True)
    start_col = jnp.sum(jnp.where(lane < sub, rows_row, 0), axis=1, keepdims=True)
    target_col = jnp.sum(jnp.where(hot, owner_start, 0), axis=1, keepdims=True)
    at = iota((count, total), 1)
    inside = (at >= start_col) & (at < start_col + rows_col)
    shift = jnp.sum(jnp.where(inside, target_col - start_col, 0), axis=0, keepdims=True)
    target = iota((1, total), 1) + shift
    pick = jnp.where(iota((total, total), 0) == target, 1.0, 0.0).astype(bf16)
    out_ref[...] = dot(pick, rows_ref[...]).astype(bf16)


def route(request_slot, new_lengths, prefill_latent):
    count = request_slot.shape[0]
    flat = new_lengths.reshape(-1)
    total, width = prefill_latent.shape
    return call(
        route_kernel,
        jax.ShapeDtypeStruct((total, width), bf16),
        (2 * total * total * width, 4 * total * width),
        name="route",
    )(
        request_slot.reshape(count, 1),
        request_slot.reshape(1, count),
        flat.reshape(count, 1),
        flat.reshape(1, count),
        prefill_latent,
    )


def reshard_kernel(tp, width, wg_ref, wu_ref, wd_ref, gu_ref, dn_ref, g_scr, u_scr, d_scr):
    block = tp * width
    units = wg_ref.shape[1]
    picker = share_picker(tp, width)
    for i in range(GROUP):
        rows = slice(i * block, (i + 1) * block)
        parts = (
            (dot(picker, wg_ref[rows, :]), g_scr),
            (dot(picker, wu_ref[rows, :]), u_scr),
            (dot(picker, wd_ref[:, rows], NT), d_scr),
        )
        for value, scratch in parts:
            value = value.astype(bf16)
            for j in range(tp):
                scratch[pl.ds((j * GROUP + i) * PAD, PAD), :] = value[j * PAD : (j + 1) * PAD, :]
    two = (2 * units, units)
    eye_g = jnp.where(iota(two, 0) == iota(two, 1), 1.0, 0.0).astype(bf16)
    eye_u = jnp.where(iota(two, 0) == iota(two, 1) + units, 1.0, 0.0).astype(bf16)
    gu = (dot(eye_g, g_scr[...], NT) + dot(eye_u, u_scr[...], NT)).astype(bf16)
    padded = (dn_ref.shape[1], units)
    eye_d = jnp.where(iota(padded, 0) == iota(padded, 1), 1.0, 0.0).astype(bf16)
    dn = dot(eye_d, d_scr[...], NT).astype(bf16)
    lanes = GROUP * PAD
    for j in range(tp):
        gu_ref[j] = gu[:, j * lanes : (j + 1) * lanes]
        dn_ref[j] = dn[:, j * lanes : (j + 1) * lanes]


def reshard(w_gate, w_up, w_down, dp, tp, width, unit_pad):
    units = w_gate.shape[1]
    block = tp * width * GROUP
    lanes = GROUP * PAD
    scratch = pltpu.VMEM((tp * lanes, units), bf16)
    return call(
        functools.partial(reshard_kernel, tp, width),
        (
            jax.ShapeDtypeStruct((tp, 2 * units, dp * PAD), bf16),
            jax.ShapeDtypeStruct((tp, unit_pad, dp * PAD), bf16),
        ),
        (2 * 3 * dp * tp * PAD * tp * width * units, 14 * w_gate.size),
        grid=(dp // GROUP,),
        in_specs=[
            pl.BlockSpec((block, units), lambda c: (c, 0)),
            pl.BlockSpec((block, units), lambda c: (c, 0)),
            pl.BlockSpec((units, block), lambda c: (0, c)),
        ],
        out_specs=(
            pl.BlockSpec((tp, 2 * units, lanes), lambda c: (0, 0, c)),
            pl.BlockSpec((tp, unit_pad, lanes), lambda c: (0, 0, c)),
        ),
        scratch_shapes=[scratch, scratch, scratch],
        name="reshard",
    )(w_gate, w_up, w_down)


def turn_kernel(x_ref, out_ref):
    lanes = x_ref.shape[1]
    eye = jnp.where(iota((lanes, lanes), 0) == iota((lanes, lanes), 1), 1.0, 0.0).astype(bf16)
    out_ref[...] = dot(eye, x_ref[...], NT).astype(bf16)


def turn(x):
    rows, columns = x.shape
    lanes = 256 if columns % 256 == 0 else 128
    return call(
        turn_kernel,
        jax.ShapeDtypeStruct((columns, rows), bf16),
        (2 * lanes * rows * columns, 4 * rows * columns),
        grid=(columns // lanes,),
        in_specs=[pl.BlockSpec((rows, lanes), lambda c: (0, c))],
        out_specs=pl.BlockSpec((lanes, rows), lambda c: (c, 0)),
        name="turn",
    )(x)


def wout_kernel(tp, width, w_ref, out_ref):
    out_ref[...] = dot(share_picker(tp, width), w_ref[0], NT).astype(bf16)


def turn_wout(w_out, tp, width):
    heads, values, columns = w_out.shape
    return call(
        functools.partial(wout_kernel, tp, width),
        jax.ShapeDtypeStruct((tp * PAD, heads * values), bf16),
        (2 * tp * PAD * columns * heads * values, 4 * w_out.size),
        grid=(heads,),
        in_specs=[pl.BlockSpec((1, values, columns), lambda h: (h, 0, 0))],
        out_specs=pl.BlockSpec((tp * PAD, values), lambda h: (0, h)),
        name="turn_wout",
    )(w_out)


def hidden_kernel(dp, per_owner, steps, h_ref, out_ref):
    total, width = h_ref.shape
    eye = jnp.where(iota((PAD, width), 0) == iota((PAD, width), 1), 1.0, 0.0).astype(bf16)
    turned = dot(eye, h_ref[...], NT).astype(bf16)
    out_ref[...] = dot(turned, token_picker(dp, per_owner, steps))


def cache_kernel(ctx_ref, q_ref, kv_ref, tok_ref, acc_ref, top_ref, sum_ref):
    at = pl.program_id(0)
    scale = QKD ** (-0.5)
    steps, _, heads, width = q_ref.shape
    rows = steps * heads
    query = q_ref[...].reshape(rows, width)
    keys = kv_ref[0]
    toks = tok_ref[0]
    scores = dot(query, keys, NT) * scale
    scores = jnp.where(iota(scores.shape, 1) < ctx_ref[at], scores, masked_score)
    fresh = dot(query, toks, NT) * scale
    step = iota(fresh.shape, 0) // heads
    fresh = jnp.where(iota(fresh.shape, 1) <= step, fresh, masked_score)
    top = jnp.maximum(
        jnp.max(scores, axis=1, keepdims=True), jnp.max(fresh, axis=1, keepdims=True)
    )
    scores = jnp.exp(scores - top)
    fresh = jnp.exp(fresh - top)
    total = jnp.sum(scores, axis=1, keepdims=True) + jnp.sum(fresh, axis=1, keepdims=True)
    acc_ref[0] = dot(scores.astype(bf16), keys[:, :LAT]) + dot(fresh.astype(bf16), toks[:, :LAT])
    top_ref[0] = jnp.broadcast_to(top, top_ref.shape[1:])
    sum_ref[0] = jnp.broadcast_to(total, sum_ref.shape[1:])


def attend_cache(ctx_lengths, queries, kv_cache, tokens):
    steps, per_owner, heads, width = queries.shape
    keys = kv_cache.shape[1]
    rows = steps * heads
    side = jax.ShapeDtypeStruct((per_owner, rows, 128), f32)
    side_spec = pl.BlockSpec((1, rows, 128), lambda q: (q, 0, 0))
    return call(
        cache_kernel,
        (jax.ShapeDtypeStruct((per_owner, rows, LAT), f32), side, side),
        (2 * per_owner * rows * keys * (width + LAT), 2 * kv_cache.size),
        grid=(per_owner,),
        in_specs=[
            pl.BlockSpec(memory_space=pltpu.SMEM),
            pl.BlockSpec((steps, 1, heads, width), lambda q: (0, q, 0, 0)),
            pl.BlockSpec((1, keys, width), lambda q: (q, 0, 0)),
            pl.BlockSpec((1, tokens.shape[1], width), lambda q: (q, 0, 0)),
        ],
        out_specs=(pl.BlockSpec((1, rows, LAT), lambda q: (q, 0, 0)), side_spec, side_spec),
        name="attend_cache",
    )(ctx_lengths, queries, kv_cache, tokens)


def merge_kernel(len_ref, q_ref, new_ref, acc_ref, top_ref, sum_ref, uv_ref, out_ref):
    scale = QKD ** (-0.5)
    steps, per_owner, heads, width = q_ref.shape
    rows = steps * heads
    new = new_ref[...]
    query = jnp.concatenate([q_ref[:, q].reshape(rows, width) for q in range(per_owner)], axis=0)
    scores = dot(query, new, NT) * scale
    place = iota(scores.shape, 1) % OWN_TOK
    owner_row = iota(scores.shape, 0) // rows
    first = jnp.zeros(scores.shape, i32)
    last = jnp.zeros(scores.shape, i32)
    start = jnp.int32(0)
    for q in range(per_owner):
        end = start + len_ref[q]
        first = jnp.where(owner_row == q, start, first)
        last = jnp.where(owner_row == q, end, last)
        start = end
    scores = jnp.where((place >= first) & (place < last), scores, masked_score)
    total_rows = per_owner * rows
    old_top = top_ref[...].reshape(total_rows, 128)[:, :1]
    old_sum = sum_ref[...].reshape(total_rows, 128)[:, :1]
    top = jnp.maximum(jnp.max(scores, axis=1, keepdims=True), old_top)
    scores = jnp.exp(scores - top)
    weight = jnp.exp(old_top - top)
    total = jnp.sum(scores, axis=1, keepdims=True) + old_sum * weight
    acc = acc_ref[...].reshape(total_rows, LAT) * weight + dot(scores.astype(bf16), new[:, :LAT])
    latent = (acc / total).astype(bf16)
    values = uv_ref.shape[2]
    groups = per_owner * steps
    head_of = iota((groups, heads, values), 1)
    for h in range(heads):
        full = dot(latent, uv_ref[h]).reshape(groups, heads, values)
        mine = jnp.sum(jnp.where(head_of == h, full, 0.0), axis=1).astype(bf16)
        out_ref[:, :, h * values : (h + 1) * values] = jnp.broadcast_to(
            mine[None], (out_ref.shape[0], groups, values)
        )


def attend_new(my_lengths, queries, new_rows, acc, top, total, w_uv, dp):
    steps, per_owner, heads, _ = queries.shape
    whole = pl.BlockSpec(memory_space=pltpu.VMEM)
    return call(
        merge_kernel,
        jax.ShapeDtypeStruct((dp, per_owner * steps, heads * w_uv.shape[2]), bf16),
        (4 * new_rows.size * per_owner * steps * heads, 2 * w_uv.size),
        in_specs=[pl.BlockSpec(memory_space=pltpu.SMEM)] + [whole] * 6,
        out_specs=whole,
        name="attend_new",
    )(my_lengths, queries, new_rows, acc, top, total, w_uv)


def project_kernel(w_ref, x_ref, out_ref):
    out_ref[...] = dot(w_ref[...], x_ref[...], NT).astype(bf16).reshape(out_ref.shape)


def project(turned, every, tp):
    rows, depth = turned.shape
    return call(
        project_kernel,
        jax.ShapeDtypeStruct((tp, PAD, every.shape[0]), bf16),
        (2 * rows * depth * every.shape[0], 2 * (turned.size + every.size)),
        name="project",
    )(turned, every)


def split_sum(value):
    high = value.astype(bf16).astype(f32)
    return high, value - high


def mixed_kernel(width, part_ref, hidden_ref, gain_ref, mixed_ref, out_ref):
    mixed = jnp.sum(part_ref[...].astype(f32), axis=0) + hidden_ref[...]
    mixed_ref[...] = mixed
    high, low = split_sum(jnp.sum(mixed * mixed, axis=0, keepdims=True))
    row = iota(mixed.shape, 0)
    sent = jnp.where(row == width, high, jnp.where(row == width + 1, low, mixed * gain_ref[...]))
    out_ref[...] = jnp.broadcast_to(sent.astype(bf16)[None], out_ref.shape)


def make_mixed(parts, hidden_t, gain, dp, width):
    _, rows, columns = parts.shape
    return call(
        functools.partial(mixed_kernel, width),
        (
            jax.ShapeDtypeStruct((rows, columns), f32),
            jax.ShapeDtypeStruct((dp, rows, columns), bf16),
        ),
        (parts.size, 4 * parts.size),
        name="make_mixed",
    )(parts, hidden_t, gain)


def gate_kernel(width, w_ref, x_ref, out_ref):
    units = w_ref.shape[1]
    x = x_ref[...]
    depth = x.shape[0]
    extra = out_ref.shape[1] - units
    place = iota((extra, depth), 1) % PAD
    pick = jnp.where((place == width) | (place == width + 1), 1.0, 0.0).astype(bf16)
    squares = dot(pick, x)
    high, low = split_sum(squares)
    row = iota(squares.shape, 0)
    tail = jnp.where(row == 0, high, jnp.where(row == 1, low, 0.0))
    out_ref[0, :units, :] = dot(w_ref[0], x).astype(bf16)
    out_ref[0, units:, :] = tail.astype(bf16)


def gate_up(weights, x, width):
    tp, units, depth = weights.shape
    columns = x.shape[1]
    return call(
        functools.partial(gate_kernel, width),
        jax.ShapeDtypeStruct((tp, units + 16, columns), bf16),
        (2 * weights.size * columns, 2 * weights.size + 2 * x.size),
        grid=(tp,),
        in_specs=[
            pl.BlockSpec((1, units, depth), lambda j: (j, 0, 0)),
            pl.BlockSpec((depth, columns), lambda j: (0, 0)),
        ],
        out_specs=pl.BlockSpec((1, units + 16, columns), lambda j: (j, 0, 0)),
        name="gate_up",
    )(weights, x)


def activate_kernel(model_width, units, part_ref, out_ref):
    sums = jnp.sum(part_ref[...].astype(f32), axis=0)
    squares = sums[2 * units : 2 * units + 1] + sums[2 * units + 1 : 2 * units + 2]
    factor = lax.rsqrt(squares / model_width + norm_eps)
    gate = sums[:units] * factor
    up = sums[units : 2 * units] * factor
    value = gate / (1.0 + jnp.exp(-gate)) * up
    spare = out_ref.shape[1] - units
    if spare:
        value = jnp.concatenate([value, jnp.zeros((spare, value.shape[1]), f32)], axis=0)
    out_ref[...] = jnp.broadcast_to(value.astype(bf16)[None], out_ref.shape)


def activate(parts, model_width, units, unit_pad):
    tp, _, columns = parts.shape
    return call(
        functools.partial(activate_kernel, model_width, units),
        jax.ShapeDtypeStruct((tp, unit_pad, columns), bf16),
        (10 * parts.size, 4 * parts.size),
        name="activate",
    )(parts)


def down_kernel(w_ref, x_ref, out_ref):
    out_ref[...] = dot(w_ref[...], x_ref[...]).astype(bf16).reshape(out_ref.shape)


def down(turned, x, dp):
    rows, depth = turned.shape
    columns = x.shape[1]
    block = 256 if rows % 256 == 0 else 128
    return call(
        down_kernel,
        jax.ShapeDtypeStruct((dp, PAD, columns), bf16),
        (2 * turned.size * columns, 2 * turned.size + 2 * x.size),
        grid=(rows // block,),
        in_specs=[
            pl.BlockSpec((block, depth), lambda c: (c, 0)),
            pl.BlockSpec((depth, columns), lambda c: (0, 0)),
        ],
        out_specs=pl.BlockSpec((block // PAD, PAD, columns), lambda c: (c, 0, 0)),
        name="down",
    )(turned, x)


def finish_kernel(dp, per_owner, steps, part_ref, mixed_ref, out_ref):
    value = jnp.sum(part_ref[...].astype(f32), axis=0) + mixed_ref[...]
    picked = dot(token_picker(dp, per_owner, steps), value.astype(bf16), NT)
    out_ref[...] = picked[:, : out_ref.shape[1]].astype(bf16)


def exchange(x, axis):
    return lax.all_to_all(x, axis, split_axis=0, concat_axis=0, tiled=True)


def shards(
    prefill_latent,
    request_slot,
    new_lengths,
    ctx_lengths,
    kv_cache,
    queries,
    step_latents,
    w_uv,
    w_out,
    hidden,
    ffn_gain,
    w_gate,
    w_up,
    w_down,
):
    dp, tp = lax.axis_size("dp"), lax.axis_size("tp")
    dp_rank, tp_rank = lax.axis_index("dp"), lax.axis_index("tp")
    steps, per_owner = queries.shape[:2]
    width = hidden.shape[2]
    model_width = width * dp * tp
    units = w_gate.shape[1]
    unit_pad = -(-units // 16) * 16
    total = hidden.shape[0] * hidden.shape[1]

    routed = route(request_slot, new_lengths, prefill_latent)
    incoming = exchange(routed.reshape(dp, OWN_TOK, -1), "dp").reshape(dp * OWN_TOK, -1)

    tokens = jnp.pad(step_latents.transpose(1, 0, 2), ((0, 0), (0, 16 - steps), (0, 0)))
    acc, top, sums = attend_cache(ctx_lengths, queries, kv_cache, tokens)

    gate_up_w, down_w = reshard(w_gate, w_up, w_down, dp, tp, width, unit_pad)
    gate_up_w = exchange(gate_up_w, "tp")
    down_w = exchange(down_w, "tp")
    turned_out = turn_wout(w_out, tp, width)
    hidden_t = call(
        functools.partial(hidden_kernel, dp, per_owner, steps),
        jax.ShapeDtypeStruct((PAD, total), f32),
        name="turn_hidden",
    )(hidden.reshape(total, width))
    gain = lax.dynamic_slice_in_dim(ffn_gain, (dp_rank * tp + tp_rank) * width, width)
    gain = jnp.pad(gain, (0, PAD - width)).reshape(PAD, 1)

    my_lengths = lax.dynamic_index_in_dim(new_lengths, dp_rank, 0, keepdims=False)
    heads_out = attend_new(my_lengths, queries, incoming, acc, top, sums, w_uv, dp)
    every = exchange(heads_out, "dp").reshape(total, -1)
    parts = exchange(project(turned_out, every, tp), "tp")
    mixed, sent = make_mixed(parts, hidden_t, gain, dp, width)
    x = exchange(sent, "dp").reshape(dp * PAD, total)
    parts = exchange(gate_up(gate_up_w, x, width), "tp")
    act = exchange(activate(parts, model_width, units, unit_pad), "tp").reshape(-1, total)
    turned_down = turn(down_w.reshape(tp * unit_pad, dp * PAD))
    parts = exchange(down(turned_down, act, dp), "dp")
    out = call(
        functools.partial(finish_kernel, dp, per_owner, steps),
        jax.ShapeDtypeStruct((total, width), bf16),
        name="finish",
    )(parts, mixed)
    return out.reshape(steps, -1, width)


def solution(mesh):
    return jax.shard_map(
        shards,
        mesh=mesh,
        in_specs=(
            P("dp", None),
            P(),
            P(),
            P("dp"),
            P("dp", None, None),
            P(None, "dp", "tp", None),
            P(None, "dp", None),
            P("tp", None, None),
            P("tp", None, "dp"),
            P(None, None, ("dp", "tp")),
            P(),
            P(None, ("dp", "tp")),
            P(None, ("dp", "tp")),
            P(("dp", "tp"), None),
        ),
        out_specs=P(None, None, ("dp", "tp")),
        check_vma=False,
    )
```

```python
import functools

import jax
import jax.numpy as jnp
from jax import lax
from jax.experimental import pallas as pl
from jax.experimental.pallas import tpu as pltpu
from jax.sharding import PartitionSpec as P

LAT = 512
QKD = 192
OWN_TOK = 16
PAD = 32
GROUP = 4

masked_score = -1e30
norm_eps = 1e-06
bf16, f32, i32 = jnp.bfloat16, jnp.float32, jnp.int32

NT = (((1,), (1,)), ((), ()))
NN = (((1,), (0,)), ((), ()))


def dot(a, b, dims=NN):
    return lax.dot_general(a, b, dims, preferred_element_type=f32)


def iota(shape, dim):
    return lax.broadcasted_iota(i32, shape, dim)


def call(body, out_shape, cost=(0, 0), mib=16, **kwargs):
    return pl.pallas_call(
        body,
        out_shape=out_shape,
        compiler_params=pltpu.CompilerParams(vmem_limit_bytes=mib * 1024 * 1024),
        cost_estimate=pl.CostEstimate(flops=cost[0], bytes_accessed=cost[1], transcendentals=0),
        **kwargs,
    )


def in_hbm(x):
    return pltpu.with_memory_space_constraint(x, pltpu.HBM)


def share_picker(tp, width):
    shape = (tp * PAD, tp * width)
    row = iota(shape, 0)
    place = row % PAD
    wanted = (row // PAD) * width + place
    return jnp.where((iota(shape, 1) == wanted) & (place < width), 1.0, 0.0).astype(bf16)


def partner(rank, tp, k, sign):
    x = (rank // 2 + sign * (k // 2) + tp // 2) % (tp // 2)
    return 2 * x + ((rank % 2) ^ (k % 2))


def token_picker(dp, per_owner, steps):
    total = dp * per_owner * steps
    shape = (total, total)
    row = iota(shape, 0)
    step, request = row // (dp * per_owner), row % (dp * per_owner)
    wanted = request * steps + step
    return jnp.where(iota(shape, 1) == wanted, 1.0, 0.0).astype(bf16)


def route_kernel(slot_ref, len_ref, rows_ref, out_ref):
    count = slot_ref.shape[1]
    per_owner, owners = len_ref.shape
    total = rows_ref.shape[1]
    square = (count, count)
    sub, lane = iota(square, 0), iota(square, 1)
    slot_row = slot_ref[...]
    spread = jnp.where(iota((owners, count), 1) // per_owner == iota((owners, count), 0), 1.0, 0.0)
    wide = dot(len_ref[...].astype(f32).astype(bf16), spread.astype(bf16))
    own = iota(wide.shape, 1) % per_owner == iota(wide.shape, 0)
    len_row = jnp.sum(jnp.where(own, wide, 0.0), axis=0, keepdims=True).astype(i32)
    len_col = jnp.sum(jnp.where(sub == lane, len_row, 0), axis=1, keepdims=True)
    slot_col = jnp.sum(jnp.where(sub == lane, slot_row, 0), axis=1, keepdims=True)
    hot = slot_col == lane
    hot_t = sub == slot_row
    rows_col = jnp.sum(jnp.where(hot, len_row, 0), axis=1, keepdims=True)
    rows_row = jnp.sum(jnp.where(hot_t, len_col, 0), axis=0, keepdims=True)
    owner_start = jnp.sum(jnp.where(sub < lane, len_col, 0), axis=0, keepdims=True)
    start_col = jnp.sum(jnp.where(lane < sub, rows_row, 0), axis=1, keepdims=True)
    target_col = jnp.sum(jnp.where(hot, owner_start, 0), axis=1, keepdims=True)
    at = iota((count, total), 1)
    inside = (at >= start_col) & (at < start_col + rows_col)
    shift = jnp.sum(jnp.where(inside, target_col - start_col, 0), axis=0, keepdims=True)
    target = iota((1, total), 1) + shift
    pick = jnp.where(iota((total, total), 0) == target, 1.0, 0.0).astype(bf16)
    out_ref[...] = dot(pick, rows_ref[...], NT).astype(bf16)


def route(request_slot, new_lengths, prefill_latent):
    total, width = prefill_latent.shape
    return call(
        route_kernel,
        jax.ShapeDtypeStruct((total, width), bf16),
        (2 * total * total * width, 4 * total * width),
        grid=(1,),
        in_specs=[
            pl.BlockSpec((1, request_slot.size), lambda c: (0, 0)),
            pl.BlockSpec(new_lengths.shape[::-1], lambda c: (0, 0)),
            pl.BlockSpec((width, total), lambda c: (0, 0)),
        ],
        out_specs=pl.BlockSpec((total, width), lambda c: (0, 0)),
        name="route",
    )(in_hbm(request_slot.reshape(1, -1)), in_hbm(new_lengths.T), in_hbm(prefill_latent.T))


def piece_places(tp):
    arrays = [(0,), (1,), (2, 3), (6, 7), (4,), (5,)]
    arrays = [[k for k in ks if k < tp] for ks in arrays]
    arrays = [ks for ks in arrays if ks]
    return {k: (n, at) for n, ks in enumerate(arrays) for at, k in enumerate(ks)}


def reshard_kernel(tp, width, rank_ref, wg_ref, wu_ref, wd_ref, *refs):
    *outs, all_scr, sorted_scr = refs
    block = tp * width
    units = wg_ref.shape[0]
    picker = share_picker(tp, width)
    lanes = GROUP * PAD
    all_scr[3 * units :, :] = jnp.zeros((all_scr.shape[0] - 3 * units, all_scr.shape[1]), bf16)
    for n, w_ref in enumerate((wg_ref, wu_ref, wd_ref)):
        all_scr[n * units : (n + 1) * units, :] = w_ref[...]
    places = piece_places(tp)
    for u in range(outs[0].shape[1]):
        picked = [
            dot(all_scr[:, i * block : (i + 1) * block], picker, NT).astype(bf16)
            for i in range(u * GROUP, (u + 1) * GROUP)
        ]
        for j in range(tp):
            part = [value[:, j * PAD : (j + 1) * PAD] for value in picked]
            sorted_scr[u, :, j * lanes : (j + 1) * lanes] = jnp.concatenate(part, axis=1)
        for k in range(tp):
            first = pl.multiple_of(partner(rank_ref[0], tp, k, 1) * lanes, lanes)
            array, at = places[k]
            outs[array][at, u] = sorted_scr[u, :, pl.ds(first, lanes)]


def reshard(rank, w_gate, w_up, w_down, dp, tp, width, unit_pad):
    units = w_gate.shape[1]
    count = dp // GROUP
    each = count // 2 if count % 2 == 0 else count
    block = tp * width * GROUP * each
    lanes = GROUP * PAD
    rows = 2 * units + unit_pad
    w_spec = pl.BlockSpec((units, block), lambda c: (0, c))
    places = piece_places(tp)
    owners = [n for n, _ in places.values()]
    sizes = [owners.count(n) for n in range(max(owners) + 1)]
    return call(
        functools.partial(reshard_kernel, tp, width),
        tuple(pltpu.HBM((size, count, rows, lanes), bf16) for size in sizes),
        (2 * 3 * dp * tp * PAD * tp * width * units, 14 * w_gate.size),
        grid=(count // each,),
        in_specs=[pl.BlockSpec(memory_space=pltpu.SMEM), w_spec, w_spec, w_spec],
        out_specs=tuple(
            pl.BlockSpec((size, each, rows, lanes), lambda c: (0, c, 0, 0)) for size in sizes
        ),
        scratch_shapes=[
            pltpu.VMEM((rows, block), bf16),
            pltpu.VMEM((each, rows, tp * lanes), bf16),
        ],
        name="reshard",
        mib=24,
    )(rank, in_hbm(w_gate.T), in_hbm(w_up.T), in_hbm(w_down))


def turn_kernel(first, *refs):
    _, count, _, lanes = refs[0].shape
    eye = jnp.where(iota((lanes, lanes), 0) == iota((lanes, lanes), 1), 1.0, 0.0).astype(bf16)
    for c in range(count):
        x = jnp.concatenate([ref[0, c, first:, :] for ref in refs[:-1]], axis=0)
        refs[-1][c * lanes : (c + 1) * lanes, :] = dot(eye, x, NT).astype(bf16)


def turn(pieces, first):
    _, count, rows, lanes = pieces[0][0].shape
    depth = len(pieces) * (rows - first)
    each = 4 if count % 4 == 0 else 1
    return call(
        functools.partial(turn_kernel, first),
        jax.ShapeDtypeStruct((count * lanes, depth), bf16),
        (2 * lanes * lanes * depth * count, 4 * depth * lanes * count),
        grid=(count // each,),
        in_specs=[
            pl.BlockSpec((1, each, rows, lanes), lambda c, at=at: (at, c, 0, 0)) for _, at in pieces
        ],
        out_specs=pl.BlockSpec((each * lanes, depth), lambda c: (c, 0)),
        name="turn",
    )(*[in_hbm(array) for array, _ in pieces])


def hidden_kernel(dp, per_owner, steps, h_ref, out_ref):
    width = h_ref.shape[0]
    eye = jnp.where(iota((PAD, width), 0) == iota((PAD, width), 1), 1.0, 0.0).astype(bf16)
    placed = dot(h_ref[...], token_picker(dp, per_owner, steps)).astype(bf16)
    out_ref[...] = dot(eye, placed)


def cache_kernel(ctx_ref, q_ref, kv_ref, tok_ref, acc_ref, side_ref):
    at = pl.program_id(0)
    scale = QKD ** (-0.5)
    steps, _, heads, width = q_ref.shape
    rows = steps * heads
    query = q_ref[...].reshape(rows, width)
    keys = kv_ref[0]
    toks = tok_ref[0]
    scores = dot(query, keys) * scale
    scores = jnp.where(iota(scores.shape, 1) < ctx_ref[at], scores, masked_score)
    fresh = dot(query, toks, NT) * scale
    step = iota(fresh.shape, 0) // heads
    fresh = jnp.where(iota(fresh.shape, 1) <= step, fresh, masked_score)
    top = jnp.maximum(
        jnp.max(scores, axis=1, keepdims=True), jnp.max(fresh, axis=1, keepdims=True)
    )
    scores = jnp.exp(scores - top)
    fresh = jnp.exp(fresh - top)
    total = jnp.sum(scores, axis=1, keepdims=True) + jnp.sum(fresh, axis=1, keepdims=True)
    acc_ref[0] = dot(scores.astype(bf16), keys[:LAT], NT) + dot(fresh.astype(bf16), toks[:, :LAT])
    side_ref[0] = jnp.where(iota(side_ref.shape[1:], 1) == 0, top, total)


def attend_cache(ctx_lengths, queries, kv_cache, tokens):
    steps, per_owner, heads, width = queries.shape
    keys = kv_cache.shape[2]
    rows = steps * heads
    side_spec = pl.BlockSpec((1, rows, 128), lambda q: (q, 0, 0))
    return call(
        cache_kernel,
        (pltpu.HBM((per_owner, rows, LAT), f32), pltpu.HBM((per_owner, rows, 128), f32)),
        (2 * per_owner * rows * keys * (width + LAT), 2 * kv_cache.size),
        grid=(per_owner,),
        in_specs=[
            pl.BlockSpec(memory_space=pltpu.SMEM),
            pl.BlockSpec((steps, 1, heads, width), lambda q: (0, q, 0, 0)),
            pl.BlockSpec((1, width, keys), lambda q: (q, 0, 0)),
            pl.BlockSpec((1, tokens.shape[1], width), lambda q: (q, 0, 0)),
        ],
        out_specs=(pl.BlockSpec((1, rows, LAT), lambda q: (q, 0, 0)), side_spec),
        name="attend_cache",
    )(ctx_lengths, queries, kv_cache, tokens)


def merge_kernel(len_ref, q_ref, new_ref, acc_ref, side_ref, uv_ref, out_ref):
    scale = QKD ** (-0.5)
    steps, per_owner, heads, width = q_ref.shape
    rows = steps * heads
    new = new_ref[...]
    query = jnp.concatenate([q_ref[:, q].reshape(rows, width) for q in range(per_owner)], axis=0)
    scores = dot(query, new, NT) * scale
    place = iota(scores.shape, 1) % OWN_TOK
    owner_row = iota(scores.shape, 0) // rows
    first = jnp.zeros(scores.shape, i32)
    last = jnp.zeros(scores.shape, i32)
    start = jnp.int32(0)
    for q in range(per_owner):
        end = start + len_ref[q]
        first = jnp.where(owner_row == q, start, first)
        last = jnp.where(owner_row == q, end, last)
        start = end
    scores = jnp.where((place >= first) & (place < last), scores, masked_score)
    total_rows = per_owner * rows
    side = side_ref[...].reshape(total_rows, 128)
    old_top, old_sum = side[:, :1], side[:, 1:2]
    top = jnp.maximum(jnp.max(scores, axis=1, keepdims=True), old_top)
    scores = jnp.exp(scores - top)
    weight = jnp.exp(old_top - top)
    total = jnp.sum(scores, axis=1, keepdims=True) + old_sum * weight
    acc = acc_ref[...].reshape(total_rows, LAT) * weight + dot(scores.astype(bf16), new[:, :LAT])
    latent = (acc / total).astype(bf16)
    values = uv_ref.shape[2]
    groups = per_owner * steps
    head_of = iota((groups, heads, values), 1)
    for h in range(heads):
        full = dot(latent, uv_ref[h]).reshape(groups, heads, values)
        mine = jnp.sum(jnp.where(head_of == h, full, 0.0), axis=1).astype(bf16)
        each = out_ref.shape[3] // values
        place = (h % each) * values
        out_ref[:, h // each, :, place : place + values] = jnp.broadcast_to(
            mine[None], (out_ref.shape[0], groups, values)
        )


def attend_new(my_lengths, queries, new_rows, acc, side, w_uv, dp, parts):
    steps, per_owner, heads, _ = queries.shape
    whole = pl.BlockSpec(memory_space=pltpu.VMEM)
    return call(
        merge_kernel,
        jax.ShapeDtypeStruct(
            (dp // parts, parts, per_owner * steps, heads // parts * w_uv.shape[2]), bf16
        ),
        (4 * new_rows.size * per_owner * steps * heads, 2 * w_uv.size),
        grid=(1,),
        in_specs=[
            pl.BlockSpec(memory_space=pltpu.SMEM),
            whole,
            whole,
            pl.BlockSpec(acc.shape, lambda c: (0, 0, 0)),
            pl.BlockSpec(side.shape, lambda c: (0, 0, 0)),
            whole,
        ],
        out_specs=whole,
        name="attend_new",
    )(my_lengths, queries, new_rows, in_hbm(acc), in_hbm(side), w_uv)


def project_kernel(rank_ref, x_ref, *refs):
    out_ref = refs[-1]
    ring, tp = out_ref.shape[:2]
    x = x_ref[...].T
    for k, w_ref in enumerate(refs[:-1]):
        heads, columns, _ = w_ref.shape
        width = columns // tp
        weights = jnp.concatenate([w_ref[h] for h in range(heads)], axis=1)
        value = dot(weights, x)
        spare = jnp.zeros((PAD - width, value.shape[1]), f32)
        target = (rank_ref[0] + ring - k) % ring
        for j in range(tp):
            part = jnp.concatenate([value[j * width : (j + 1) * width], spare], axis=0)
            out_ref[target, j] = part.astype(bf16)


def project(rank, pieces, every, tp):
    heads, features, values = pieces[0].shape
    ring, columns = len(pieces), every.shape[0]
    size = ring * heads * features * values
    return call(
        project_kernel,
        jax.ShapeDtypeStruct((ring, tp, PAD, columns), bf16),
        (2 * size * columns, 2 * (size + every.size)),
        grid=(1,),
        in_specs=[
            pl.BlockSpec(memory_space=pltpu.SMEM),
            pl.BlockSpec(every.shape, lambda c: (0, 0)),
        ]
        + [pl.BlockSpec((heads, features, values), lambda c: (0, 0, 0))] * ring,
        out_specs=pl.BlockSpec((ring, tp, PAD, columns), lambda c: (0, 0, 0, 0)),
        name="project",
    )(rank, every, *[in_hbm(piece) for piece in pieces])


def split_sum(value):
    high = value.astype(bf16).astype(f32)
    return high, value - high


def mixed_kernel(width, part_ref, hidden_ref, gain_ref, mixed_ref, out_ref):
    mixed = jnp.sum(part_ref[...].astype(f32), axis=0) + hidden_ref[...]
    mixed_ref[...] = mixed
    high, low = split_sum(jnp.sum(mixed * mixed, axis=0, keepdims=True))
    row = iota(mixed.shape, 0)
    sent = jnp.where(row == width, high, jnp.where(row == width + 1, low, mixed * gain_ref[...]))
    out_ref[...] = jnp.broadcast_to(sent.astype(bf16)[None], out_ref.shape)


def make_mixed(parts, hidden_t, gain, dp, width):
    _, rows, columns = parts.shape
    return call(
        functools.partial(mixed_kernel, width),
        (
            jax.ShapeDtypeStruct((rows, columns), f32),
            jax.ShapeDtypeStruct((dp, rows, columns), bf16),
        ),
        (parts.size, 4 * parts.size),
        name="make_mixed",
    )(parts, hidden_t, gain)


def gate_kernel(width, rank_ref, x_ref, *refs):
    out_ref = refs[-1]
    units = out_ref.shape[1] - 16
    x = x_ref[...]
    depth = x.shape[0]
    place = iota((16, depth), 1) % PAD
    pick = jnp.where((place == width) | (place == width + 1), 1.0, 0.0).astype(bf16)
    squares = dot(pick, x)
    high, low = split_sum(squares)
    row = iota(squares.shape, 0)
    tail = jnp.where(row == 0, high, jnp.where(row == 1, low, 0.0)).astype(bf16)
    for k, w_ref in enumerate(refs[:-1]):
        target = partner(rank_ref[0], len(refs) - 1, k, -1)
        weights = jnp.concatenate([w_ref[0, c] for c in range(w_ref.shape[1])], axis=1)
        out_ref[target, :units, :] = dot(weights, x).astype(bf16)
        out_ref[target, units:, :] = tail


def gate_up(rank, pieces, x, units, width):
    tp, columns = len(pieces), x.shape[1]
    _, count, _, lanes = pieces[0][0].shape
    size = tp * units * x.shape[0]
    out_shape = (tp, units + 16, columns)
    return call(
        functools.partial(gate_kernel, width),
        jax.ShapeDtypeStruct(out_shape, bf16),
        (2 * size * columns, 2 * size + 2 * x.size),
        grid=(1,),
        in_specs=[
            pl.BlockSpec(memory_space=pltpu.SMEM),
            pl.BlockSpec(x.shape, lambda c: (0, 0)),
        ]
        + [
            pl.BlockSpec((1, count, units, lanes), lambda c, at=at: (at, 0, 0, 0)) for _, at in pieces
        ],
        out_specs=pl.BlockSpec(out_shape, lambda c: (0, 0, 0)),
        name="gate_up",
    )(rank, x, *[in_hbm(array) for array, _ in pieces])


def activate_kernel(model_width, units, part_ref, out_ref):
    sums = jnp.sum(part_ref[...].astype(f32), axis=0)
    squares = sums[2 * units : 2 * units + 1] + sums[2 * units + 1 : 2 * units + 2]
    factor = lax.rsqrt(squares / model_width + norm_eps)
    gate = sums[:units] * factor
    up = sums[units : 2 * units] * factor
    value = gate / (1.0 + jnp.exp(-gate)) * up
    spare = out_ref.shape[1] - units
    if spare:
        value = jnp.concatenate([value, jnp.zeros((spare, value.shape[1]), f32)], axis=0)
    out_ref[...] = jnp.broadcast_to(value.astype(bf16)[None], out_ref.shape)


def activate(parts, model_width, units, unit_pad):
    tp, _, columns = parts.shape
    return call(
        functools.partial(activate_kernel, model_width, units),
        jax.ShapeDtypeStruct((tp, unit_pad, columns), bf16),
        (10 * parts.size, 4 * parts.size),
        name="activate",
    )(parts)


def down_kernel(rank_ref, w_ref, x_ref, out_ref):
    tp = x_ref.shape[0]
    x = jnp.concatenate([x_ref[partner(rank_ref[0], tp, k, -1)] for k in range(tp)], axis=0)
    out_ref[...] = dot(w_ref[...], x).astype(bf16).reshape(out_ref.shape)


def down(rank, turned, x, dp):
    rows, depth = turned.shape
    columns = x.shape[2]
    block = 256 if rows % 256 == 0 else 128
    return call(
        down_kernel,
        jax.ShapeDtypeStruct((dp, PAD, columns), bf16),
        (2 * turned.size * columns, 2 * turned.size + 2 * x.size),
        grid=(rows // block,),
        in_specs=[
            pl.BlockSpec(memory_space=pltpu.SMEM),
            pl.BlockSpec((block, depth), lambda c: (c, 0)),
            pl.BlockSpec(x.shape, lambda c: (0, 0, 0)),
        ],
        out_specs=pl.BlockSpec((block // PAD, PAD, columns), lambda c: (c, 0, 0)),
        name="down",
    )(rank, turned, x)


def finish_kernel(dp, per_owner, steps, part_ref, mixed_ref, out_ref):
    value = jnp.sum(part_ref[...].astype(f32), axis=0) + mixed_ref[...]
    picked = dot(value.astype(bf16), token_picker(dp, per_owner, steps), NT)
    picked = picked[: out_ref.shape[0]].astype(bf16)
    each = out_ref.shape[2]
    for s in range(steps):
        out_ref[:, s, :] = picked[:, s * each : (s + 1) * each]


def exchange(x, axis):
    return lax.all_to_all(x, axis, split_axis=0, concat_axis=0, tiled=True)


def shards(
    prefill_latent,
    request_slot,
    new_lengths,
    ctx_lengths,
    kv_cache,
    queries,
    step_latents,
    w_uv,
    w_out,
    hidden,
    ffn_gain,
    w_gate,
    w_up,
    w_down,
):
    both = ("z", "y")
    ring = lax.axis_size("y")
    dp, tp = lax.axis_size("z") * ring, lax.axis_size("tp")
    dp_rank, tp_rank = lax.axis_index(both), lax.axis_index("tp")
    steps, per_owner = queries.shape[:2]
    width = hidden.shape[2]
    model_width = width * dp * tp
    units = w_gate.shape[1]
    unit_pad = -(-units // 16) * 16
    total = hidden.shape[0] * hidden.shape[1]

    routed = route(request_slot, new_lengths, prefill_latent)
    incoming = exchange(routed.reshape(dp, OWN_TOK, -1), both).reshape(dp * OWN_TOK, -1)

    rank = tp_rank.astype(i32).reshape(1)
    arrays = reshard(rank, w_gate, w_up, w_down, dp, tp, width, unit_pad)

    ctx_lengths, _ = lax.optimization_barrier((ctx_lengths, arrays[0]))
    tokens = jnp.pad(step_latents.transpose(1, 0, 2), ((0, 0), (0, 16 - steps), (0, 0)))
    acc, side = attend_cache(
        ctx_lengths, queries, in_hbm(kv_cache.transpose(0, 2, 1)), tokens
    )
    my_lengths = lax.dynamic_index_in_dim(new_lengths, dp_rank, 0, keepdims=False)
    heads_out = attend_new(my_lengths, queries, incoming, acc, side, w_uv, dp, ring)
    every = exchange(heads_out.reshape((dp,) + heads_out.shape[2:]), both).reshape(total, -1)

    def along_x(piece, k, sign):
        return lax.ppermute(piece, "tp", [(j, partner(j, tp, k, sign)) for j in range(tp)])

    y_rank = lax.axis_index("y").astype(i32).reshape(1)
    each = w_out.shape[0] // ring
    w_turned = w_out.transpose(0, 2, 1)
    out_pieces = [
        lax.dynamic_slice_in_dim(w_turned, (y_rank[0] + k) % ring * each, each, 0)
        for k in range(ring)
    ]
    for k in range(1, ring):
        pairs = [(j, (j + k) % ring) for j in range(ring)]
        out_pieces[k] = lax.ppermute(out_pieces[k], "y", pairs)
    pieces = {k: (arrays[n], at) for k, (n, at) in piece_places(tp).items()}
    if tp > 2:
        plus, minus = along_x(arrays[2], 2, 1), along_x(arrays[3], 2, -1)
        far, _ = lax.optimization_barrier((arrays[4:6], (plus, minus)))
        far = [along_x(far[0], 2, 1), along_x(far[1], 2, -1)]
        every, _ = lax.optimization_barrier((every, (plus, minus, far)))
    parts = project(y_rank, out_pieces, every, tp)
    parts = exchange(parts.reshape((ring * tp,) + parts.shape[2:]), ("y", "tp"))
    if tp > 2:
        pieces[2], pieces[6] = (plus, 0), (minus, 0)
        pieces[3] = along_x(plus[1:], 1, 1), 0
        pieces[7] = along_x(minus[1:], 1, 1), 0
        pieces[4] = along_x(far[0], 2, 1), 0
        pieces[5] = along_x(far[1], 3, -1), 0
    pieces[1] = along_x(arrays[1], 1, 1), 0
    pieces = [pieces[k] for k in range(tp)]
    hidden_t = call(
        functools.partial(hidden_kernel, dp, per_owner, steps),
        jax.ShapeDtypeStruct((PAD, total), f32),
        name="turn_hidden",
    )(hidden.transpose(2, 0, 1).reshape(width, total))
    gain = lax.dynamic_slice_in_dim(ffn_gain, (dp_rank * tp + tp_rank) * width, width)
    gain = jnp.pad(gain, (0, PAD - width)).reshape(PAD, 1)

    mixed, sent = make_mixed(parts, hidden_t, gain, dp, width)
    x = exchange(sent, both).reshape(dp * PAD, total)
    parts = exchange(gate_up(rank, pieces, x, 2 * units, width), "tp")
    act = exchange(activate(parts, model_width, units, unit_pad), "tp")
    turned_down = turn(pieces, 2 * units)
    parts = exchange(down(rank, turned_down, act, dp), both)
    out = call(
        functools.partial(finish_kernel, dp, per_owner, steps),
        jax.ShapeDtypeStruct((width, steps, total // steps), bf16),
        name="finish",
    )(parts, mixed)
    return out.transpose(1, 2, 0)


def solution(mesh):
    devices = mesh.devices
    ring = 2
    devices = devices.reshape(devices.shape[0] // ring, ring, devices.shape[1])
    dp, tp = ("z", "y"), "tp"
    every = ("z", "y", "tp")
    return jax.shard_map(
        shards,
        mesh=jax.sharding.Mesh(devices, every),
        in_specs=(
            P(dp, None),
            P(),
            P(),
            P(dp),
            P(dp, None, None),
            P(None, dp, tp, None),
            P(None, dp, None),
            P(tp, None, None),
            P(tp, None, dp),
            P(None, None, every),
            P(),
            P(None, every),
            P(None, every),
            P(every, None),
        ),
        out_specs=P(None, None, every),
        check_vma=False,
    )
```

```python
import functools

import jax
import jax.numpy as jnp
from jax import lax
from jax.experimental import pallas as pl
from jax.experimental.pallas import tpu as pltpu
from jax.sharding import PartitionSpec as P

LAT = 512
QKD = 192
OWN_TOK = 16
PAD = 32
GROUP = 4

masked_score = -1e30
norm_eps = 1e-06
bf16, f32, i32 = jnp.bfloat16, jnp.float32, jnp.int32

NT = (((1,), (1,)), ((), ()))
NN = (((1,), (0,)), ((), ()))


def dot(a, b, dims=NN):
    return lax.dot_general(a, b, dims, preferred_element_type=f32)


def iota(shape, dim):
    return lax.broadcasted_iota(i32, shape, dim)


def call(body, out_shape, cost=(0, 0), mib=16, **kwargs):
    return pl.pallas_call(
        body,
        out_shape=out_shape,
        compiler_params=pltpu.CompilerParams(vmem_limit_bytes=mib * 1024 * 1024),
        cost_estimate=pl.CostEstimate(flops=cost[0], bytes_accessed=cost[1], transcendentals=0),
        **kwargs,
    )


def in_hbm(x):
    return pltpu.with_memory_space_constraint(x, pltpu.HBM)


def share_picker(tp, width, turn):
    shape = (tp * width, -(-tp // GROUP) * GROUP * PAD)
    column = iota(shape, 1)
    place = column % PAD
    slot = (column // PAD) % GROUP
    rank = column // (GROUP * PAD) * GROUP + (slot + GROUP - turn) % GROUP
    hit = (iota(shape, 0) == rank * width + place) & (place < width)
    return jnp.where(hit, 1.0, 0.0).astype(bf16)


def source_in_group(rank, slot):
    return (slot + GROUP - rank % GROUP) % GROUP


def partner(rank, tp, k, sign):
    x = (rank // 2 + sign * (k // 2) + tp // 2) % (tp // 2)
    return 2 * x + ((rank % 2) ^ (k % 2))


def token_picker(dp, per_owner, steps):
    total = dp * per_owner * steps
    shape = (total, total)
    row = iota(shape, 0)
    step, request = row // (dp * per_owner), row % (dp * per_owner)
    wanted = request * steps + step
    return jnp.where(iota(shape, 1) == wanted, 1.0, 0.0).astype(bf16)


def route_kernel(slot_ref, len_ref, rows_ref, out_ref):
    count = slot_ref.shape[1]
    per_owner, owners = len_ref.shape
    total = rows_ref.shape[1]
    square = (count, count)
    sub, lane = iota(square, 0), iota(square, 1)
    slot_row = slot_ref[...]
    spread = jnp.where(iota((owners, count), 1) // per_owner == iota((owners, count), 0), 1.0, 0.0)
    wide = dot(len_ref[...].astype(f32).astype(bf16), spread.astype(bf16))
    own = iota(wide.shape, 1) % per_owner == iota(wide.shape, 0)
    len_row = jnp.sum(jnp.where(own, wide, 0.0), axis=0, keepdims=True).astype(i32)
    len_col = jnp.sum(jnp.where(sub == lane, len_row, 0), axis=1, keepdims=True)
    slot_col = jnp.sum(jnp.where(sub == lane, slot_row, 0), axis=1, keepdims=True)
    hot = slot_col == lane
    hot_t = sub == slot_row
    rows_col = jnp.sum(jnp.where(hot, len_row, 0), axis=1, keepdims=True)
    rows_row = jnp.sum(jnp.where(hot_t, len_col, 0), axis=0, keepdims=True)
    owner_start = jnp.sum(jnp.where(sub < lane, len_col, 0), axis=0, keepdims=True)
    start_col = jnp.sum(jnp.where(lane < sub, rows_row, 0), axis=1, keepdims=True)
    target_col = jnp.sum(jnp.where(hot, owner_start, 0), axis=1, keepdims=True)
    at = iota((count, total), 1)
    inside = (at >= start_col) & (at < start_col + rows_col)
    shift = jnp.sum(jnp.where(inside, target_col - start_col, 0), axis=0, keepdims=True)
    target = iota((1, total), 1) + shift
    pick = jnp.where(iota((total, total), 0) == target, 1.0, 0.0).astype(bf16)
    out_ref[...] = dot(pick, rows_ref[...], NT).astype(bf16)


def route(request_slot, new_lengths, prefill_latent):
    total, width = prefill_latent.shape
    return call(
        route_kernel,
        jax.ShapeDtypeStruct((total, width), bf16),
        (2 * total * total * width, 4 * total * width),
        grid=(1,),
        in_specs=[
            pl.BlockSpec((1, request_slot.size), lambda c: (0, 0)),
            pl.BlockSpec(new_lengths.shape[::-1], lambda c: (0, 0)),
            pl.BlockSpec((width, total), lambda c: (0, 0)),
        ],
        out_specs=pl.BlockSpec((total, width), lambda c: (0, 0)),
        name="route",
    )(in_hbm(request_slot.reshape(1, -1)), in_hbm(new_lengths.T), in_hbm(prefill_latent.T))


def piece_places(tp):
    arrays = [(0,), (1,), (2, 3), (6, 7), (4,), (5,)]
    arrays = [[k for k in ks if k < tp] for ks in arrays]
    arrays = [ks for ks in arrays if ks]
    return {k: (n, at) for n, ks in enumerate(arrays) for at, k in enumerate(ks)}


def reshard_kernel(tp, width, rank_ref, gain_ref, wg_ref, wu_ref, wd_ref, *refs):
    *outs, all_scr, pick_scr, sort_scr = refs
    block = tp * width
    units = wg_ref.shape[0]
    lanes = GROUP * PAD

    @pl.when(pl.program_id(0) == 0)
    def _():
        for i in range(GROUP):
            pick_scr[i] = share_picker(tp, width, i)
        all_scr[3 * units :, :] = jnp.zeros((all_scr.shape[0] - 3 * units, all_scr.shape[1]), bf16)

    for n, w_ref in enumerate((wg_ref, wu_ref, wd_ref)):
        value = w_ref[...]
        if n < 2:
            value = (value.astype(f32) * gain_ref[...]).astype(bf16)
        all_scr[n * units : (n + 1) * units, :] = value
    slot_of = iota((all_scr.shape[0], lanes), 1) // PAD
    places = piece_places(tp)
    for u in range(outs[0].shape[1]):
        for i in range(GROUP):
            first = (u * GROUP + i) * block
            sort_scr[u, i] = dot(all_scr[:, first : first + block], pick_scr[i]).astype(bf16)
        for k in range(tp):
            target = partner(rank_ref[0], tp, k, 1)
            tile = pl.multiple_of(target // GROUP * lanes, lanes)
            value = None
            for slot in range(GROUP):
                part = sort_scr[u, source_in_group(target, slot), :, pl.ds(tile, lanes)]
                value = part if value is None else jnp.where(slot_of == slot, part, value)
            array, at = places[k]
            outs[array][at, u] = value


def reshard(rank, gain, w_gate, w_up, w_down, dp, tp, width, unit_pad):
    units = w_gate.shape[1]
    count = dp // GROUP
    each = 2 if count % 2 == 0 else 1
    block = tp * width * GROUP * each
    lanes = GROUP * PAD
    rows = 2 * units + unit_pad
    w_spec = pl.BlockSpec((units, block), lambda c: (0, c))
    tiles = -(-tp // GROUP)
    places = piece_places(tp)
    owners = [n for n, _ in places.values()]
    sizes = [owners.count(n) for n in range(max(owners) + 1)]
    return call(
        functools.partial(reshard_kernel, tp, width),
        tuple(pltpu.HBM((size, count, rows, lanes), bf16) for size in sizes),
        (2 * 3 * dp * tp * PAD * tp * width * units, 14 * w_gate.size),
        grid=(count // each,),
        in_specs=[
            pl.BlockSpec(memory_space=pltpu.SMEM),
            pl.BlockSpec((1, block), lambda c: (0, c)),
            w_spec,
            w_spec,
            w_spec,
        ],
        out_specs=tuple(
            pl.BlockSpec((size, each, rows, lanes), lambda c: (0, c, 0, 0)) for size in sizes
        ),
        scratch_shapes=[
            pltpu.VMEM((rows, block), bf16),
            pltpu.VMEM((GROUP, tp * width, tiles * lanes), bf16),
            pltpu.VMEM((each, GROUP, rows, tiles * lanes), bf16),
        ],
        name="reshard",
        mib=24,
    )(rank, gain.reshape(1, -1), in_hbm(w_gate.T), in_hbm(w_up.T), in_hbm(w_down))


def turn_kernel(first, *refs):
    _, count, _, lanes = refs[0].shape
    eye = jnp.where(iota((lanes, lanes), 0) == iota((lanes, lanes), 1), 1.0, 0.0).astype(bf16)
    for c in range(count):
        x = jnp.concatenate([ref[0, c, first:, :] for ref in refs[:-1]], axis=0)
        refs[-1][c * lanes : (c + 1) * lanes, :] = dot(eye, x, NT).astype(bf16)


def turn(pieces, places, first):
    _, count, rows, lanes = pieces[0][0].shape
    depth = len(pieces) * (rows - first)
    each = 4 if count % 4 == 0 else 1
    return call(
        functools.partial(turn_kernel, first),
        jax.ShapeDtypeStruct((count * lanes, depth), bf16),
        (2 * lanes * lanes * depth * count, 4 * depth * lanes * count),
        grid=(count // each,),
        in_specs=[
            pl.BlockSpec((1, each, rows, lanes), lambda c, at=at: (at, c, 0, 0)) for _, at in pieces
        ],
        out_specs=pl.BlockSpec((each * lanes, depth), lambda c: (c, 0)),
        name="turn",
    )(*[place(array) for (array, _), place in zip(pieces, places)])


def hidden_kernel(dp, per_owner, steps, h_ref, out_ref):
    width = h_ref.shape[0]
    eye = jnp.where(iota((PAD, width), 0) == iota((PAD, width), 1), 1.0, 0.0).astype(bf16)
    placed = dot(h_ref[...], token_picker(dp, per_owner, steps)).astype(bf16)
    out_ref[...] = dot(eye, placed)


def cache_kernel(ctx_ref, q_ref, kv_ref, tok_ref, acc_ref, side_ref):
    at = pl.program_id(0)
    scale = QKD ** (-0.5)
    steps, _, heads, width = q_ref.shape
    rows = steps * heads
    query = q_ref[...].reshape(rows, width)
    keys = kv_ref[0]
    toks = tok_ref[0]
    scores = dot(query, keys) * scale
    scores = jnp.where(iota(scores.shape, 1) < ctx_ref[at], scores, masked_score)
    fresh = dot(query, toks, NT) * scale
    step = iota(fresh.shape, 0) // heads
    fresh = jnp.where(iota(fresh.shape, 1) <= step, fresh, masked_score)
    top = jnp.maximum(
        jnp.max(scores, axis=1, keepdims=True), jnp.max(fresh, axis=1, keepdims=True)
    )
    scores = jnp.exp(scores - top)
    fresh = jnp.exp(fresh - top)
    total = jnp.sum(scores, axis=1, keepdims=True) + jnp.sum(fresh, axis=1, keepdims=True)
    acc_ref[0] = dot(scores.astype(bf16), keys[:LAT], NT) + dot(fresh.astype(bf16), toks[:, :LAT])
    side_ref[0] = jnp.where(iota(side_ref.shape[1:], 1) == 0, top, total)


def attend_cache(ctx_lengths, queries, kv_cache, tokens):
    steps, per_owner, heads, width = queries.shape
    keys = kv_cache.shape[2]
    rows = steps * heads
    side_spec = pl.BlockSpec((1, rows, 128), lambda q: (q, 0, 0))
    return call(
        cache_kernel,
        (pltpu.HBM((per_owner, rows, LAT), f32), pltpu.HBM((per_owner, rows, 128), f32)),
        (2 * per_owner * rows * keys * (width + LAT), 2 * kv_cache.size),
        grid=(per_owner,),
        in_specs=[
            pl.BlockSpec(memory_space=pltpu.SMEM),
            pl.BlockSpec((steps, 1, heads, width), lambda q: (0, q, 0, 0)),
            pl.BlockSpec((1, width, keys), lambda q: (q, 0, 0)),
            pl.BlockSpec((1, tokens.shape[1], width), lambda q: (q, 0, 0)),
        ],
        out_specs=(pl.BlockSpec((1, rows, LAT), lambda q: (q, 0, 0)), side_spec),
        name="attend_cache",
    )(ctx_lengths, queries, kv_cache, tokens)


def merge_kernel(len_ref, q_ref, new_ref, acc_ref, side_ref, uv_ref, out_ref):
    scale = QKD ** (-0.5)
    steps, per_owner, heads, width = q_ref.shape
    rows = steps * heads
    new = new_ref[...]
    query = jnp.concatenate([q_ref[:, q].reshape(rows, width) for q in range(per_owner)], axis=0)
    scores = dot(query, new, NT) * scale
    place = iota(scores.shape, 1) % OWN_TOK
    owner_row = iota(scores.shape, 0) // rows
    first = jnp.zeros(scores.shape, i32)
    last = jnp.zeros(scores.shape, i32)
    start = jnp.int32(0)
    for q in range(per_owner):
        end = start + len_ref[q]
        first = jnp.where(owner_row == q, start, first)
        last = jnp.where(owner_row == q, end, last)
        start = end
    scores = jnp.where((place >= first) & (place < last), scores, masked_score)
    total_rows = per_owner * rows
    side = side_ref[...].reshape(total_rows, 128)
    old_top, old_sum = side[:, :1], side[:, 1:2]
    top = jnp.maximum(jnp.max(scores, axis=1, keepdims=True), old_top)
    scores = jnp.exp(scores - top)
    weight = jnp.exp(old_top - top)
    total = jnp.sum(scores, axis=1, keepdims=True) + old_sum * weight
    acc = acc_ref[...].reshape(total_rows, LAT) * weight + dot(scores.astype(bf16), new[:, :LAT])
    latent = (acc / total).astype(bf16)
    values = uv_ref.shape[2]
    groups = per_owner * steps
    each = out_ref.shape[3] // values
    for h in range(0, heads, 2):
        full = dot(latent, jnp.concatenate([uv_ref[h], uv_ref[h + 1]], axis=1))
        full = full.reshape(groups, heads, 2 * values)
        wanted = h + iota(full.shape, 2) // values
        mine = jnp.sum(jnp.where(iota(full.shape, 1) == wanted, full, 0.0), axis=1).astype(bf16)
        place = (h % each) * values
        out_ref[:, h // each, :, place : place + 2 * values] = jnp.broadcast_to(
            mine[None], (out_ref.shape[0], groups, 2 * values)
        )


def attend_new(my_lengths, queries, new_rows, acc, side, w_uv, dp, parts):
    steps, per_owner, heads, _ = queries.shape
    whole = pl.BlockSpec(memory_space=pltpu.VMEM)
    return call(
        merge_kernel,
        jax.ShapeDtypeStruct(
            (dp // parts, parts, per_owner * steps, heads // parts * w_uv.shape[2]), bf16
        ),
        (4 * new_rows.size * per_owner * steps * heads, 2 * w_uv.size),
        grid=(1,),
        in_specs=[
            pl.BlockSpec(memory_space=pltpu.SMEM),
            whole,
            whole,
            pl.BlockSpec(acc.shape, lambda c: (0, 0, 0)),
            pl.BlockSpec(side.shape, lambda c: (0, 0, 0)),
            whole,
        ],
        out_specs=whole,
        name="attend_new",
    )(my_lengths, queries, new_rows, in_hbm(acc), in_hbm(side), w_uv)


def gather_heads_kernel(rank_ref, *refs):
    out_ref = refs[-1]
    ring = len(refs) - 1
    for k, w_ref in enumerate(refs[:-1]):
        heads, _, values = w_ref.shape
        target = (rank_ref[0] + ring - k) % ring
        for h in range(heads):
            out_ref[target, :, h * values : (h + 1) * values] = w_ref[h]


def gather_heads(rank, own, pieces):
    heads, features, values = pieces[0].shape
    ring = 1 + len(pieces)
    block = (heads, features, values)
    return call(
        gather_heads_kernel,
        jax.ShapeDtypeStruct((ring, features, heads * values), bf16),
        (0, 4 * ring * heads * features * values),
        grid_spec=pltpu.PrefetchScalarGridSpec(
            num_scalar_prefetch=1,
            grid=(1,),
            in_specs=[pl.BlockSpec(block, lambda c, rank: (rank[0], 0, 0))]
            + [pl.BlockSpec(block, lambda c, rank: (0, 0, 0))] * len(pieces),
            out_specs=pl.BlockSpec(memory_space=pltpu.VMEM),
        ),
        name="gather_heads",
    )(rank, in_hbm(own), *[in_hbm(piece) for piece in pieces])


def project_kernel(w_ref, x_ref, out_ref):
    ring, tp = out_ref.shape[:2]
    x = x_ref[...].T
    for n in range(ring):
        width = w_ref.shape[1] // tp
        value = dot(w_ref[n], x)
        spare = jnp.zeros((PAD - width, value.shape[1]), f32)
        for j in range(tp):
            part = jnp.concatenate([value[j * width : (j + 1) * width], spare], axis=0)
            out_ref[n, j] = part.astype(bf16)


def project(weights, every, tp):
    ring, features, depth = weights.shape
    columns = every.shape[0]
    whole = pl.BlockSpec(memory_space=pltpu.VMEM)
    return call(
        project_kernel,
        jax.ShapeDtypeStruct((ring, tp, PAD, columns), bf16),
        (2 * weights.size * columns, 2 * (weights.size + every.size)),
        in_specs=[whole, whole],
        out_specs=whole,
        name="project",
    )(weights, every)


def split_sum(value):
    high = value.astype(bf16).astype(f32)
    return high, value - high


def stack_halves(value, width):
    half = value.shape[1] // 2
    return jnp.concatenate([value[:width, :half], value[:width, half:]], axis=0)


def mixed_kernel(width, part_ref, hidden_ref, mixed_ref, out_ref):
    mixed = jnp.sum(part_ref[...].astype(f32), axis=0) + hidden_ref[...]
    mixed_ref[...] = mixed
    sent = stack_halves(mixed, width).astype(bf16)
    out_ref[...] = jnp.broadcast_to(sent[None], out_ref.shape)


def make_mixed(parts, hidden_t, dp, width):
    _, rows, columns = parts.shape
    return call(
        functools.partial(mixed_kernel, width),
        (
            jax.ShapeDtypeStruct((rows, columns), f32),
            jax.ShapeDtypeStruct((dp, 2 * width, columns // 2), bf16),
        ),
        (parts.size, 4 * parts.size),
        name="make_mixed",
    )(parts, hidden_t)


def gate_kernel(groups, rank_ref, x_ref, *refs):
    *w_refs, keep_ref, send_ref = refs
    units = w_refs[0].shape[1]
    width = x_ref.shape[1] // 2
    blocks = []
    for c in range(0, x_ref.shape[0], GROUP):
        for slot in range(GROUP):
            piece = x_ref[c + source_in_group(rank_ref[0], slot)].astype(f32)
            spare = jnp.zeros((PAD - width, piece.shape[1]), f32)
            right = jnp.concatenate([piece[width:], spare], axis=0)
            blocks.append(jnp.concatenate([piece[:PAD], right], axis=1))
    x = jnp.concatenate(blocks, axis=0)
    squares = jnp.where(iota(x.shape, 0) % PAD < width, x * x, 0.0)
    high, low = split_sum(jnp.sum(squares, axis=0, keepdims=True))
    row = iota((16, x.shape[1]), 0)
    tail = jnp.where(row == 0, high, jnp.where(row == 1, low, 0.0)).astype(bf16)
    x = x.astype(bf16)
    for w_ref, group in zip(w_refs, groups):
        for at, k in enumerate(group):
            n = partner(rank_ref[0], 2 * keep_ref.shape[0], k, -1) // 2
            out_ref = send_ref if k % 2 else keep_ref
            out_ref[n, :units, :] = dot(w_ref[at], x).astype(bf16)
            out_ref[n, units:, :] = tail


def collect_kernel(*refs):
    for n, w_ref in enumerate(refs[:-1]):
        lanes = w_ref.shape[3]
        for c in range(w_ref.shape[1]):
            refs[-1][n, :, c * lanes : (c + 1) * lanes] = w_ref[0, c]


def collect(pieces, places, units):
    tp = len(pieces)
    _, count, _, lanes = pieces[0][0].shape
    out_shape = (tp, units, count * lanes)
    return call(
        collect_kernel,
        jax.ShapeDtypeStruct(out_shape, bf16),
        (0, 4 * tp * units * count * lanes),
        grid=(1,),
        in_specs=[
            pl.BlockSpec((1, count, units, lanes), lambda c, at=at: (at, 0, 0, 0)) for _, at in pieces
        ],
        out_specs=pl.BlockSpec(memory_space=pltpu.VMEM),
        name="collect",
    )(*[place(array) for (array, _), place in zip(pieces, places)])


def gate_up(rank, weights, groups, x):
    tp = sum(len(group) for group in groups)
    _, units, depth = weights[0].shape
    size = tp * units * depth
    columns = 2 * x.shape[2]
    whole = pl.BlockSpec(memory_space=pltpu.VMEM)
    out = jax.ShapeDtypeStruct((tp // 2, units + 16, columns), bf16)
    return call(
        functools.partial(gate_kernel, groups),
        (out, out),
        (2 * size * columns, 2 * size + 2 * x.size),
        in_specs=[pl.BlockSpec(memory_space=pltpu.SMEM)] + [whole] * (1 + len(weights)),
        out_specs=(whole, whole),
        name="gate_up",
    )(rank, x, *weights)


def add_kernel(units, a_ref, b_ref, out_ref):
    out_ref[:, :units, :] = (
        a_ref[:, :units, :].astype(f32) + b_ref[:, :units, :].astype(f32)
    ).astype(bf16)
    tail = a_ref[:, units:, :].astype(f32) + b_ref[:, units:, :].astype(f32)
    high, low = split_sum(tail[:, 0:1] + tail[:, 1:2])
    row = iota(tail.shape, 1)
    tail = jnp.where(row == 0, high, jnp.where(row == 1, low, 0.0))
    out_ref[:, units:, :] = tail.astype(bf16)


def add_cores(a, b, units):
    return call(
        functools.partial(add_kernel, units),
        jax.ShapeDtypeStruct(a.shape, bf16),
        (2 * a.size, 6 * a.size),
        name="add_cores",
    )(a, b)


def activate_kernel(model_width, units, part_ref, out_ref):
    sums = jnp.sum(part_ref[...].astype(f32), axis=0)
    squares = sums[2 * units : 2 * units + 1] + sums[2 * units + 1 : 2 * units + 2]
    factor = lax.rsqrt(squares / model_width + norm_eps)
    gate = sums[:units] * factor
    up = sums[units : 2 * units] * factor
    value = gate / (1.0 + jnp.exp(-gate)) * up
    spare = out_ref.shape[1] - units
    if spare:
        value = jnp.concatenate([value, jnp.zeros((spare, value.shape[1]), f32)], axis=0)
    out_ref[...] = jnp.broadcast_to(value.astype(bf16)[None], out_ref.shape)


def activate(parts, model_width, units, unit_pad):
    tp, _, columns = parts.shape
    return call(
        functools.partial(activate_kernel, model_width, units),
        jax.ShapeDtypeStruct((tp, unit_pad, columns), bf16),
        (10 * parts.size, 4 * parts.size),
        name="activate",
    )(parts)


def down_kernel(rank_ref, w_ref, same_ref, other_ref, out_ref):
    tp = 2 * same_ref.shape[0]
    refs = (same_ref, other_ref)
    sources = [partner(rank_ref[0], tp, k, -1) // 2 for k in range(tp)]
    x = jnp.concatenate([refs[k % 2][n] for k, n in enumerate(sources)], axis=0)
    value = dot(w_ref[...], x)
    count, rows, _ = out_ref.shape
    value = value.reshape(count, PAD, value.shape[1])
    for n in range(count):
        first, slot = n // GROUP * GROUP, n % GROUP
        out_ref[first + source_in_group(rank_ref[0], slot)] = stack_halves(
            value[n], rows // 2
        ).astype(bf16)


def down(rank, turned, same, other, dp, width):
    rows, depth = turned.shape
    columns = same.shape[2]
    block = 256 if rows % 256 == 0 else 128
    x_spec = pl.BlockSpec(same.shape, lambda c: (0, 0, 0))
    return call(
        down_kernel,
        jax.ShapeDtypeStruct((dp, 2 * width, columns // 2), bf16),
        (2 * turned.size * columns, 2 * turned.size + 4 * same.size),
        grid=(rows // block,),
        in_specs=[
            pl.BlockSpec(memory_space=pltpu.SMEM),
            pl.BlockSpec((block, depth), lambda c: (c, 0)),
            x_spec,
            x_spec,
        ],
        out_specs=pl.BlockSpec((block // PAD, 2 * width, columns // 2), lambda c: (c, 0, 0)),
        name="down",
    )(rank, turned, same, other)


def finish_kernel(dp, per_owner, steps, part_ref, mixed_ref, out_ref):
    value = jnp.sum(part_ref[...].astype(f32), axis=0)
    width = value.shape[0] // 2
    value = jnp.concatenate([value[:width], value[width:]], axis=1) + mixed_ref[:width]
    picked = dot(value.astype(bf16), token_picker(dp, per_owner, steps), NT)
    picked = picked.astype(bf16)
    each = out_ref.shape[2]
    for s in range(steps):
        out_ref[:, s, :] = picked[:, s * each : (s + 1) * each]


def exchange(x, axis, groups=None):
    return lax.all_to_all(
        x, axis, split_axis=0, concat_axis=0, tiled=True, axis_index_groups=groups
    )


def swap_cores(x):
    return lax.ppermute(x, "tp", [(j, j ^ 1) for j in range(lax.axis_size("tp"))])


def shards(
    prefill_latent,
    request_slot,
    new_lengths,
    ctx_lengths,
    kv_cache,
    queries,
    step_latents,
    w_uv,
    w_out,
    hidden,
    ffn_gain,
    w_gate,
    w_up,
    w_down,
):
    both = ("z", "y")
    ring = lax.axis_size("y")
    dp, tp = lax.axis_size("z") * ring, lax.axis_size("tp")
    dp_rank, tp_rank = lax.axis_index(both), lax.axis_index("tp")
    steps, per_owner = queries.shape[:2]
    width = hidden.shape[2]
    model_width = width * dp * tp
    units = w_gate.shape[1]
    unit_pad = -(-units // 16) * 16
    total = hidden.shape[0] * hidden.shape[1]

    routed = route(request_slot, new_lengths, prefill_latent)
    incoming = exchange(routed.reshape(dp, OWN_TOK, -1), both).reshape(dp * OWN_TOK, -1)

    rank = tp_rank.astype(i32).reshape(1)
    arrays = reshard(rank, ffn_gain, w_gate, w_up, w_down, dp, tp, width, unit_pad)

    y_rank = lax.axis_index("y").astype(i32).reshape(1)
    each = w_out.shape[0] // ring
    w_turned = w_out.transpose(0, 2, 1)
    out_pieces = []
    for k in range(1, ring):
        piece = lax.dynamic_slice_in_dim(w_turned, (y_rank[0] + k) % ring * each, each, 0)
        pairs = [(j, (j + k) % ring) for j in range(ring)]
        out_pieces.append(lax.ppermute(piece, "y", pairs))
    incoming, _ = lax.optimization_barrier((incoming, out_pieces))

    ctx_lengths, _ = lax.optimization_barrier((ctx_lengths, arrays[0]))
    tokens = jnp.pad(step_latents.transpose(1, 0, 2), ((0, 0), (0, 16 - steps), (0, 0)))
    acc, side = attend_cache(
        ctx_lengths, queries, in_hbm(kv_cache.transpose(0, 2, 1)), tokens
    )
    my_lengths = lax.dynamic_index_in_dim(new_lengths, dp_rank, 0, keepdims=False)
    heads_out = attend_new(my_lengths, queries, incoming, acc, side, w_uv, dp, ring)
    every = exchange(heads_out.reshape((dp,) + heads_out.shape[2:]), both).reshape(total, -1)

    def along_x(piece, k, sign):
        return lax.ppermute(piece, "tp", [(j, partner(j, tp, k, sign)) for j in range(tp)])

    pieces = {k: (arrays[n], at) for k, (n, at) in piece_places(tp).items()}
    if tp > 2:
        plus, minus = along_x(arrays[2], 2, 1), along_x(arrays[3], 2, -1)
        far, _ = lax.optimization_barrier((arrays[4:6], (plus, minus)))
        far = [along_x(far[0], 2, 1), along_x(far[1], 2, -1)]
        every, _ = lax.optimization_barrier((every, (plus, minus, far)))
    parts = project(gather_heads(y_rank, w_turned, out_pieces), every, tp)
    parts = exchange(parts.reshape((ring * tp,) + parts.shape[2:]), ("y", "tp"))
    if tp > 2:
        pieces[2], pieces[6] = (plus, 0), (minus, 0)
        swapped = [along_x(plus[1:], 1, 1), along_x(minus[1:], 1, 1)]
        parts, _ = lax.optimization_barrier((parts, swapped))
        pieces[3], pieces[7] = (swapped[0], 0), (swapped[1], 0)
        pieces[4] = along_x(far[0], 2, 1), 0
        pieces[5] = along_x(far[1], 3, -1), 0
    pieces[1] = along_x(arrays[1], 1, 1), 0
    pieces = [pieces[k] for k in range(tp)]
    hidden_t = call(
        functools.partial(hidden_kernel, dp, per_owner, steps),
        jax.ShapeDtypeStruct((PAD, total), f32),
        name="turn_hidden",
    )(hidden.transpose(2, 0, 1).reshape(width, total))
    mixed, sent = make_mixed(parts, hidden_t, dp, width)
    x = exchange(sent, both)
    groups = [[k for k in range(tp) if k // 2 != 2], [k for k in range(tp) if k // 2 == 2]]
    groups = [group for group in groups if group]
    places = [(lambda array: array) if k // 2 == 2 else in_hbm for k in range(tp)]
    weights = [
        collect([pieces[k] for k in group], [places[k] for k in group], 2 * units)
        for group in groups
    ]
    keep, send = gate_up(rank, weights, groups, x)
    along = [[2 * n + core for n in range(tp // 2)] for core in range(2)]
    parts = exchange(add_cores(keep, swap_cores(send), 2 * units), "tp", along)
    parts, turned_down = lax.optimization_barrier((parts, turn(pieces, [in_hbm] * tp, 2 * units)))
    same = exchange(activate(parts, model_width, units, unit_pad), "tp", along)
    other = swap_cores(same)
    parts = exchange(down(rank, turned_down, same, other, dp, width), both)
    out = call(
        functools.partial(finish_kernel, dp, per_owner, steps),
        jax.ShapeDtypeStruct((width, steps, total // steps), bf16),
        name="finish",
    )(parts, mixed)
    return out.transpose(1, 2, 0)


def solution(mesh):
    devices = mesh.devices
    ring = 2
    devices = devices.reshape(devices.shape[0] // ring, ring, devices.shape[1])
    dp, tp = ("z", "y"), "tp"
    every = ("z", "y", "tp")
    return jax.shard_map(
        shards,
        mesh=jax.sharding.Mesh(devices, every),
        in_specs=(
            P(dp, None),
            P(),
            P(),
            P(dp),
            P(dp, None, None),
            P(None, dp, tp, None),
            P(None, dp, None),
            P(tp, None, None),
            P(tp, None, dp),
            P(None, None, every),
            P(),
            P(None, every),
            P(None, every),
            P(every, None),
        ),
        out_specs=P(None, None, every),
        check_vma=False,
    )
```

```python
import functools

import jax
import jax.numpy as jnp
from jax import lax
from jax.experimental import pallas as pl
from jax.experimental.pallas import tpu as pltpu
from jax.sharding import PartitionSpec as P

LAT = 512
QKD = 192
OWN_TOK = 16
PAD = 32
GROUP = 4

masked_score = -1e30
norm_eps = 1e-06
bf16, f32, i32 = jnp.bfloat16, jnp.float32, jnp.int32

NT = (((1,), (1,)), ((), ()))
NN = (((1,), (0,)), ((), ()))


def dot(a, b, dims=NN):
    return lax.dot_general(a, b, dims, preferred_element_type=f32)


def iota(shape, dim):
    return lax.broadcasted_iota(i32, shape, dim)


def call(body, out_shape, cost=(0, 0), mib=16, **kwargs):
    return pl.pallas_call(
        body,
        out_shape=out_shape,
        compiler_params=pltpu.CompilerParams(vmem_limit_bytes=mib * 1024 * 1024),
        cost_estimate=pl.CostEstimate(flops=cost[0], bytes_accessed=cost[1], transcendentals=0),
        **kwargs,
    )


def in_hbm(x):
    return pltpu.with_memory_space_constraint(x, pltpu.HBM)


def share_picker(tp, width, turn):
    shape = (tp * width, -(-tp // GROUP) * GROUP * PAD)
    column = iota(shape, 1)
    place = column % PAD
    slot = (column // PAD) % GROUP
    rank = column // (GROUP * PAD) * GROUP + (slot + GROUP - turn) % GROUP
    hit = (iota(shape, 0) == rank * width + place) & (place < width)
    return jnp.where(hit, 1.0, 0.0).astype(bf16)


def source_in_group(rank, slot):
    return (slot + GROUP - rank % GROUP) % GROUP


def partner(rank, tp, k, sign):
    x = (rank // 2 + sign * (k // 2) + tp // 2) % (tp // 2)
    return 2 * x + ((rank % 2) ^ (k % 2))


def token_picker(dp, per_owner, steps):
    total = dp * per_owner * steps
    shape = (total, total)
    row = iota(shape, 0)
    step, request = row // (dp * per_owner), row % (dp * per_owner)
    wanted = request * steps + step
    return jnp.where(iota(shape, 1) == wanted, 1.0, 0.0).astype(bf16)


def route_kernel(rank_ref, slot_ref, len_ref, rows_ref, out_ref):
    count = slot_ref.shape[1]
    per_owner, owners = len_ref.shape
    total = rows_ref.shape[1]
    square = (count, count)
    sub, lane = iota(square, 0), iota(square, 1)
    slot_row = slot_ref[...]
    spread = jnp.where(iota((owners, count), 1) // per_owner == iota((owners, count), 0), 1.0, 0.0)
    wide = dot(len_ref[...].astype(f32).astype(bf16), spread.astype(bf16))
    own = iota(wide.shape, 1) % per_owner == iota(wide.shape, 0)
    len_row = jnp.sum(jnp.where(own, wide, 0.0), axis=0, keepdims=True).astype(i32)
    len_col = jnp.sum(jnp.where(sub == lane, len_row, 0), axis=1, keepdims=True)
    slot_col = jnp.sum(jnp.where(sub == lane, slot_row, 0), axis=1, keepdims=True)
    hot = slot_col == lane
    hot_t = sub == slot_row
    rows_col = jnp.sum(jnp.where(hot, len_row, 0), axis=1, keepdims=True)
    rows_row = jnp.sum(jnp.where(hot_t, len_col, 0), axis=0, keepdims=True)
    owner_start = jnp.sum(jnp.where(sub < lane, len_col, 0), axis=0, keepdims=True)
    start_col = jnp.sum(jnp.where(lane < sub, rows_row, 0), axis=1, keepdims=True)
    target_col = jnp.sum(jnp.where(hot, owner_start, 0), axis=1, keepdims=True)
    at = iota((count, total), 1)
    inside = (at >= start_col) & (at < start_col + rows_col)
    shift = jnp.sum(jnp.where(inside, target_col - start_col, 0), axis=0, keepdims=True)
    target = iota((1, total), 1) + shift
    half = OWN_TOK // 2
    row = iota((total // 2, total), 0)
    wanted = row // half * OWN_TOK + rank_ref[0] % 2 * half + row % half
    pick = jnp.where(wanted == target, 1.0, 0.0).astype(bf16)
    out_ref[...] = dot(pick, rows_ref[...], NT).astype(bf16)


def route(rank, request_slot, new_lengths, prefill_latent):
    total, width = prefill_latent.shape
    return call(
        route_kernel,
        jax.ShapeDtypeStruct((total // 2, width), bf16),
        (total * total * width, 3 * total * width),
        grid=(1,),
        in_specs=[
            pl.BlockSpec(memory_space=pltpu.SMEM),
            pl.BlockSpec((1, request_slot.size), lambda c: (0, 0)),
            pl.BlockSpec(new_lengths.shape[::-1], lambda c: (0, 0)),
            pl.BlockSpec((width, total), lambda c: (0, 0)),
        ],
        out_specs=pl.BlockSpec((total // 2, width), lambda c: (0, 0)),
        name="route",
    )(rank, in_hbm(request_slot.reshape(1, -1)), in_hbm(new_lengths.T), in_hbm(prefill_latent.T))


def piece_places(tp):
    arrays = [(0,), (1,), (2, 3), (6, 7), (4,), (5,)]
    arrays = [[k for k in ks if k < tp] for ks in arrays]
    arrays = [ks for ks in arrays if ks]
    return {k: (n, at) for n, ks in enumerate(arrays) for at, k in enumerate(ks)}


def reshard_kernel(tp, width, rank_ref, gain_ref, wg_ref, wu_ref, wd_ref, *refs):
    *outs, all_scr, pick_scr, sort_scr = refs
    block = tp * width
    units = wg_ref.shape[0]
    lanes = GROUP * PAD

    @pl.when(pl.program_id(0) == 0)
    def _():
        for i in range(GROUP):
            pick_scr[i] = share_picker(tp, width, i)
        all_scr[3 * units :, :] = jnp.zeros((all_scr.shape[0] - 3 * units, all_scr.shape[1]), bf16)

    for n, w_ref in enumerate((wg_ref, wu_ref, wd_ref)):
        value = w_ref[...]
        if n < 2:
            value = (value.astype(f32) * gain_ref[...]).astype(bf16)
        all_scr[n * units : (n + 1) * units, :] = value
    slot_of = iota((all_scr.shape[0], lanes), 1) // PAD
    places = piece_places(tp)
    for u in range(outs[0].shape[1]):
        for i in range(GROUP):
            first = (u * GROUP + i) * block
            sort_scr[u, i] = dot(all_scr[:, first : first + block], pick_scr[i]).astype(bf16)
        for k in range(tp):
            target = partner(rank_ref[0], tp, k, 1)
            tile = pl.multiple_of(target // GROUP * lanes, lanes)
            value = None
            for slot in range(GROUP):
                part = sort_scr[u, source_in_group(target, slot), :, pl.ds(tile, lanes)]
                value = part if value is None else jnp.where(slot_of == slot, part, value)
            array, at = places[k]
            outs[array][at, u] = value


def reshard(rank, gain, w_gate, w_up, w_down, dp, tp, width, unit_pad):
    units = w_gate.shape[1]
    count = dp // GROUP
    each = 2 if count % 2 == 0 else 1
    block = tp * width * GROUP * each
    lanes = GROUP * PAD
    rows = 2 * units + unit_pad
    w_spec = pl.BlockSpec((units, block), lambda c: (0, c))
    tiles = -(-tp // GROUP)
    places = piece_places(tp)
    owners = [n for n, _ in places.values()]
    sizes = [owners.count(n) for n in range(max(owners) + 1)]
    return call(
        functools.partial(reshard_kernel, tp, width),
        tuple(pltpu.HBM((size, count, rows, lanes), bf16) for size in sizes),
        (2 * 3 * dp * tp * PAD * tp * width * units, 14 * w_gate.size),
        grid=(count // each,),
        in_specs=[
            pl.BlockSpec(memory_space=pltpu.SMEM),
            pl.BlockSpec((1, block), lambda c: (0, c)),
            w_spec,
            w_spec,
            w_spec,
        ],
        out_specs=tuple(
            pl.BlockSpec((size, each, rows, lanes), lambda c: (0, c, 0, 0)) for size in sizes
        ),
        scratch_shapes=[
            pltpu.VMEM((rows, block), bf16),
            pltpu.VMEM((GROUP, tp * width, tiles * lanes), bf16),
            pltpu.VMEM((each, GROUP, rows, tiles * lanes), bf16),
        ],
        name="reshard",
        mib=24,
    )(rank, gain.reshape(1, -1), in_hbm(w_gate.T), in_hbm(w_up.T), in_hbm(w_down))


def turn_kernel(first, *refs):
    _, count, _, lanes = refs[0].shape
    eye = jnp.where(iota((lanes, lanes), 0) == iota((lanes, lanes), 1), 1.0, 0.0).astype(bf16)
    for c in range(count):
        x = jnp.concatenate([ref[0, c, first:, :] for ref in refs[:-1]], axis=0)
        refs[-1][c * lanes : (c + 1) * lanes, :] = dot(eye, x, NT).astype(bf16)


def turn(pieces, places, first):
    _, count, rows, lanes = pieces[0][0].shape
    depth = len(pieces) * (rows - first)
    each = 4 if count % 4 == 0 else 1
    return call(
        functools.partial(turn_kernel, first),
        jax.ShapeDtypeStruct((count * lanes, depth), bf16),
        (2 * lanes * lanes * depth * count, 4 * depth * lanes * count),
        grid=(count // each,),
        in_specs=[
            pl.BlockSpec((1, each, rows, lanes), lambda c, at=at: (at, c, 0, 0)) for _, at in pieces
        ],
        out_specs=pl.BlockSpec((each * lanes, depth), lambda c: (c, 0)),
        name="turn",
    )(*[place(array) for (array, _), place in zip(pieces, places)])


def hidden_kernel(dp, per_owner, steps, h_ref, out_ref):
    width = h_ref.shape[0]
    eye = jnp.where(iota((PAD, width), 0) == iota((PAD, width), 1), 1.0, 0.0).astype(bf16)
    placed = dot(h_ref[...], token_picker(dp, per_owner, steps)).astype(bf16)
    out_ref[...] = dot(eye, placed)


def cache_kernel(ctx_ref, q_ref, kv_ref, tok_ref, acc_ref, side_ref):
    at = pl.program_id(0)
    scale = QKD ** (-0.5)
    steps, _, heads, width = q_ref.shape
    rows = steps * heads
    query = q_ref[...].reshape(rows, width)
    keys = kv_ref[0]
    toks = tok_ref[0]
    scores = dot(query, keys) * scale
    scores = jnp.where(iota(scores.shape, 1) < ctx_ref[at], scores, masked_score)
    fresh = dot(query, toks, NT) * scale
    step = iota(fresh.shape, 0) // heads
    fresh = jnp.where(iota(fresh.shape, 1) <= step, fresh, masked_score)
    top = jnp.maximum(
        jnp.max(scores, axis=1, keepdims=True), jnp.max(fresh, axis=1, keepdims=True)
    )
    scores = jnp.exp(scores - top)
    fresh = jnp.exp(fresh - top)
    total = jnp.sum(scores, axis=1, keepdims=True) + jnp.sum(fresh, axis=1, keepdims=True)
    acc_ref[0] = dot(scores.astype(bf16), keys[:LAT], NT) + dot(fresh.astype(bf16), toks[:, :LAT])
    side_ref[0] = jnp.where(iota(side_ref.shape[1:], 1) == 0, top, total)


def attend_cache(ctx_lengths, queries, kv_cache, tokens):
    steps, per_owner, heads, width = queries.shape
    keys = kv_cache.shape[2]
    rows = steps * heads
    side_spec = pl.BlockSpec((1, rows, 128), lambda q: (q, 0, 0))
    return call(
        cache_kernel,
        (pltpu.HBM((per_owner, rows, LAT), f32), pltpu.HBM((per_owner, rows, 128), f32)),
        (2 * per_owner * rows * keys * (width + LAT), 2 * kv_cache.size),
        grid=(per_owner,),
        in_specs=[
            pl.BlockSpec(memory_space=pltpu.SMEM),
            pl.BlockSpec((steps, 1, heads, width), lambda q: (0, q, 0, 0)),
            pl.BlockSpec((1, width, keys), lambda q: (q, 0, 0)),
            pl.BlockSpec((1, tokens.shape[1], width), lambda q: (q, 0, 0)),
        ],
        out_specs=(pl.BlockSpec((1, rows, LAT), lambda q: (q, 0, 0)), side_spec),
        name="attend_cache",
    )(ctx_lengths, queries, kv_cache, tokens)


def merge_kernel(rank_ref, len_ref, q_ref, new_ref, other_ref, acc_ref, side_ref, uv_ref, out_ref):
    scale = QKD ** (-0.5)
    steps, per_owner, heads, width = q_ref.shape
    rows = steps * heads
    new = jnp.concatenate([new_ref[...], other_ref[...]], axis=0)
    query = jnp.concatenate([q_ref[:, q].reshape(rows, width) for q in range(per_owner)], axis=0)
    scores = dot(query, new, NT) * scale
    half = OWN_TOK // 2
    column = iota(scores.shape, 1)
    core = jnp.where(column < scores.shape[1] // 2, rank_ref[0] % 2, 1 - rank_ref[0] % 2)
    place = core * half + column % half
    owner_row = iota(scores.shape, 0) // rows
    first = jnp.zeros(scores.shape, i32)
    last = jnp.zeros(scores.shape, i32)
    start = jnp.int32(0)
    for q in range(per_owner):
        end = start + len_ref[q]
        first = jnp.where(owner_row == q, start, first)
        last = jnp.where(owner_row == q, end, last)
        start = end
    scores = jnp.where((place >= first) & (place < last), scores, masked_score)
    total_rows = per_owner * rows
    side = side_ref[...].reshape(total_rows, 128)
    old_top, old_sum = side[:, :1], side[:, 1:2]
    top = jnp.maximum(jnp.max(scores, axis=1, keepdims=True), old_top)
    scores = jnp.exp(scores - top)
    weight = jnp.exp(old_top - top)
    total = jnp.sum(scores, axis=1, keepdims=True) + old_sum * weight
    acc = acc_ref[...].reshape(total_rows, LAT) * weight + dot(scores.astype(bf16), new[:, :LAT])
    latent = (acc / total).astype(bf16)
    values = uv_ref.shape[2]
    groups = per_owner * steps
    each = out_ref.shape[3] // values
    for h in range(0, heads, 2):
        full = dot(latent, jnp.concatenate([uv_ref[h], uv_ref[h + 1]], axis=1))
        full = full.reshape(groups, heads, 2 * values)
        wanted = h + iota(full.shape, 2) // values
        mine = jnp.sum(jnp.where(iota(full.shape, 1) == wanted, full, 0.0), axis=1).astype(bf16)
        place = (h % each) * values
        out_ref[:, h // each, :, place : place + 2 * values] = jnp.broadcast_to(
            mine[None], (out_ref.shape[0], groups, 2 * values)
        )


def attend_new(rank, my_lengths, queries, new_rows, other_rows, acc, side, w_uv, dp, parts):
    steps, per_owner, heads, _ = queries.shape
    whole = pl.BlockSpec(memory_space=pltpu.VMEM)
    return call(
        merge_kernel,
        jax.ShapeDtypeStruct(
            (dp // parts, parts, per_owner * steps, heads // parts * w_uv.shape[2]), bf16
        ),
        (8 * new_rows.size * per_owner * steps * heads, 2 * w_uv.size),
        grid=(1,),
        in_specs=[
            pl.BlockSpec(memory_space=pltpu.SMEM),
            pl.BlockSpec(memory_space=pltpu.SMEM),
            whole,
            whole,
            whole,
            pl.BlockSpec(acc.shape, lambda c: (0, 0, 0)),
            pl.BlockSpec(side.shape, lambda c: (0, 0, 0)),
            whole,
        ],
        out_specs=whole,
        name="attend_new",
    )(rank, my_lengths, queries, new_rows, other_rows, in_hbm(acc), in_hbm(side), w_uv)


def gather_heads_kernel(rank_ref, *refs):
    out_ref = refs[-1]
    ring = len(refs) - 1
    for k, w_ref in enumerate(refs[:-1]):
        heads, _, values = w_ref.shape
        target = (rank_ref[0] + ring - k) % ring
        for h in range(heads):
            out_ref[target, :, h * values : (h + 1) * values] = w_ref[h]


def gather_heads(rank, own, pieces):
    heads, features, values = pieces[0].shape
    ring = 1 + len(pieces)
    block = (heads, features, values)
    return call(
        gather_heads_kernel,
        jax.ShapeDtypeStruct((ring, features, heads * values), bf16),
        (0, 4 * ring * heads * features * values),
        grid_spec=pltpu.PrefetchScalarGridSpec(
            num_scalar_prefetch=1,
            grid=(1,),
            in_specs=[pl.BlockSpec(block, lambda c, rank: (rank[0], 0, 0))]
            + [pl.BlockSpec(block, lambda c, rank: (0, 0, 0))] * len(pieces),
            out_specs=pl.BlockSpec(memory_space=pltpu.VMEM),
        ),
        name="gather_heads",
    )(rank, in_hbm(own), *pieces)


def project_kernel(w_ref, x_ref, out_ref):
    ring, tp = out_ref.shape[:2]
    x = x_ref[...].T
    for n in range(ring):
        width = w_ref.shape[1] // tp
        value = dot(w_ref[n], x)
        spare = jnp.zeros((PAD - width, value.shape[1]), f32)
        for j in range(tp):
            part = jnp.concatenate([value[j * width : (j + 1) * width], spare], axis=0)
            out_ref[n, j] = part.astype(bf16)


def project(weights, every, tp):
    ring, features, depth = weights.shape
    columns = every.shape[0]
    whole = pl.BlockSpec(memory_space=pltpu.VMEM)
    return call(
        project_kernel,
        jax.ShapeDtypeStruct((ring, tp, PAD, columns), bf16),
        (2 * weights.size * columns, 2 * (weights.size + every.size)),
        in_specs=[whole, whole],
        out_specs=whole,
        name="project",
    )(weights, every)


def split_sum(value):
    high = value.astype(bf16).astype(f32)
    return high, value - high


def stack_halves(value, width):
    half = value.shape[1] // 2
    return jnp.concatenate([value[:width, :half], value[:width, half:]], axis=0)


def mixed_kernel(width, part_ref, hidden_ref, mixed_ref, out_ref):
    mixed = jnp.sum(part_ref[...].astype(f32), axis=0) + hidden_ref[...]
    mixed_ref[...] = mixed
    sent = stack_halves(mixed, width).astype(bf16)
    out_ref[...] = jnp.broadcast_to(sent[None], out_ref.shape)


def make_mixed(parts, hidden_t, dp, width):
    _, rows, columns = parts.shape
    return call(
        functools.partial(mixed_kernel, width),
        (
            jax.ShapeDtypeStruct((rows, columns), f32),
            jax.ShapeDtypeStruct((dp, 2 * width, columns // 2), bf16),
        ),
        (parts.size, 4 * parts.size),
        name="make_mixed",
    )(parts, hidden_t)


def gate_kernel(groups, rank_ref, x_ref, *refs):
    *w_refs, keep_ref, send_ref = refs
    units = w_refs[0].shape[1]
    width = x_ref.shape[1] // 2
    blocks = []
    for c in range(0, x_ref.shape[0], GROUP):
        for slot in range(GROUP):
            piece = x_ref[c + source_in_group(rank_ref[0], slot)].astype(f32)
            spare = jnp.zeros((PAD - width, piece.shape[1]), f32)
            right = jnp.concatenate([piece[width:], spare], axis=0)
            blocks.append(jnp.concatenate([piece[:PAD], right], axis=1))
    x = jnp.concatenate(blocks, axis=0)
    squares = jnp.where(iota(x.shape, 0) % PAD < width, x * x, 0.0)
    high, low = split_sum(jnp.sum(squares, axis=0, keepdims=True))
    row = iota((16, x.shape[1]), 0)
    tail = jnp.where(row == 0, high, jnp.where(row == 1, low, 0.0)).astype(bf16)
    x = x.astype(bf16)
    for w_ref, group in zip(w_refs, groups):
        for at, k in enumerate(group):
            n = partner(rank_ref[0], 2 * keep_ref.shape[0], k, -1) // 2
            out_ref = send_ref if k % 2 else keep_ref
            out_ref[n, :units, :] = dot(w_ref[at], x).astype(bf16)
            out_ref[n, units:, :] = tail


def collect_kernel(*refs):
    for n, w_ref in enumerate(refs[:-1]):
        lanes = w_ref.shape[3]
        for c in range(w_ref.shape[1]):
            refs[-1][n, :, c * lanes : (c + 1) * lanes] = w_ref[0, c]


def collect(pieces, places, units):
    tp = len(pieces)
    _, count, _, lanes = pieces[0][0].shape
    out_shape = (tp, units, count * lanes)
    return call(
        collect_kernel,
        jax.ShapeDtypeStruct(out_shape, bf16),
        (0, 4 * tp * units * count * lanes),
        grid=(1,),
        in_specs=[
            pl.BlockSpec((1, count, units, lanes), lambda c, at=at: (at, 0, 0, 0)) for _, at in pieces
        ],
        out_specs=pl.BlockSpec(memory_space=pltpu.VMEM),
        name="collect",
    )(*[place(array) for (array, _), place in zip(pieces, places)])


def gate_up(rank, weights, groups, x):
    tp = sum(len(group) for group in groups)
    _, units, depth = weights[0].shape
    size = tp * units * depth
    columns = 2 * x.shape[2]
    whole = pl.BlockSpec(memory_space=pltpu.VMEM)
    out = jax.ShapeDtypeStruct((tp // 2, units + 16, columns), bf16)
    return call(
        functools.partial(gate_kernel, groups),
        (out, out),
        (2 * size * columns, 2 * size + 2 * x.size),
        in_specs=[pl.BlockSpec(memory_space=pltpu.SMEM)] + [whole] * (1 + len(weights)),
        out_specs=(whole, whole),
        name="gate_up",
    )(rank, x, *weights)


def add_kernel(units, a_ref, b_ref, out_ref):
    out_ref[:, :units, :] = (
        a_ref[:, :units, :].astype(f32) + b_ref[:, :units, :].astype(f32)
    ).astype(bf16)
    tail = a_ref[:, units:, :].astype(f32) + b_ref[:, units:, :].astype(f32)
    high, low = split_sum(tail[:, 0:1] + tail[:, 1:2])
    row = iota(tail.shape, 1)
    tail = jnp.where(row == 0, high, jnp.where(row == 1, low, 0.0))
    out_ref[:, units:, :] = tail.astype(bf16)


def add_cores(a, b, units):
    return call(
        functools.partial(add_kernel, units),
        jax.ShapeDtypeStruct(a.shape, bf16),
        (2 * a.size, 6 * a.size),
        name="add_cores",
    )(a, b)


def activate_kernel(model_width, units, part_ref, out_ref):
    sums = jnp.sum(part_ref[...].astype(f32), axis=0)
    squares = sums[2 * units : 2 * units + 1] + sums[2 * units + 1 : 2 * units + 2]
    factor = lax.rsqrt(squares / model_width + norm_eps)
    gate = sums[:units] * factor
    up = sums[units : 2 * units] * factor
    value = gate / (1.0 + jnp.exp(-gate)) * up
    spare = out_ref.shape[1] - units
    if spare:
        value = jnp.concatenate([value, jnp.zeros((spare, value.shape[1]), f32)], axis=0)
    out_ref[...] = jnp.broadcast_to(value.astype(bf16)[None], out_ref.shape)


def activate(parts, model_width, units, unit_pad):
    tp, _, columns = parts.shape
    return call(
        functools.partial(activate_kernel, model_width, units),
        jax.ShapeDtypeStruct((tp, unit_pad, columns), bf16),
        (10 * parts.size, 4 * parts.size),
        name="activate",
    )(parts)


def down_kernel(rank_ref, w_ref, same_ref, other_ref, out_ref):
    tp = 2 * same_ref.shape[0]
    refs = (same_ref, other_ref)
    sources = [partner(rank_ref[0], tp, k, -1) // 2 for k in range(tp)]
    x = jnp.concatenate([refs[k % 2][n] for k, n in enumerate(sources)], axis=0)
    value = dot(w_ref[...], x)
    count, rows, _ = out_ref.shape
    value = value.reshape(count, PAD, value.shape[1])
    for n in range(count):
        first, slot = n // GROUP * GROUP, n % GROUP
        out_ref[first + source_in_group(rank_ref[0], slot)] = stack_halves(
            value[n], rows // 2
        ).astype(bf16)


def down(rank, turned, same, other, dp, width):
    rows, depth = turned.shape
    columns = same.shape[2]
    block = 256 if rows % 256 == 0 else 128
    x_spec = pl.BlockSpec(same.shape, lambda c: (0, 0, 0))
    return call(
        down_kernel,
        jax.ShapeDtypeStruct((dp, 2 * width, columns // 2), bf16),
        (2 * turned.size * columns, 2 * turned.size + 4 * same.size),
        grid=(rows // block,),
        in_specs=[
            pl.BlockSpec(memory_space=pltpu.SMEM),
            pl.BlockSpec((block, depth), lambda c: (c, 0)),
            x_spec,
            x_spec,
        ],
        out_specs=pl.BlockSpec((block // PAD, 2 * width, columns // 2), lambda c: (c, 0, 0)),
        name="down",
    )(rank, turned, same, other)


def finish_kernel(dp, per_owner, steps, part_ref, mixed_ref, out_ref):
    value = jnp.sum(part_ref[...].astype(f32), axis=0)
    width = value.shape[0] // 2
    value = jnp.concatenate([value[:width], value[width:]], axis=1) + mixed_ref[:width]
    picked = dot(value.astype(bf16), token_picker(dp, per_owner, steps), NT)
    picked = picked.astype(bf16)
    each = out_ref.shape[2]
    for s in range(steps):
        out_ref[:, s, :] = picked[:, s * each : (s + 1) * each]


def exchange(x, axis, groups=None):
    return lax.all_to_all(
        x, axis, split_axis=0, concat_axis=0, tiled=True, axis_index_groups=groups
    )


def swap_cores(x):
    return lax.ppermute(x, "tp", [(j, j ^ 1) for j in range(lax.axis_size("tp"))])


def shards(
    prefill_latent,
    request_slot,
    new_lengths,
    ctx_lengths,
    kv_cache,
    queries,
    step_latents,
    w_uv,
    w_out,
    hidden,
    ffn_gain,
    w_gate,
    w_up,
    w_down,
):
    both = ("z", "y")
    ring = lax.axis_size("y")
    dp, tp = lax.axis_size("z") * ring, lax.axis_size("tp")
    dp_rank, tp_rank = lax.axis_index(both), lax.axis_index("tp")
    steps, per_owner = queries.shape[:2]
    width = hidden.shape[2]
    model_width = width * dp * tp
    units = w_gate.shape[1]
    unit_pad = -(-units // 16) * 16
    total = hidden.shape[0] * hidden.shape[1]

    rank = tp_rank.astype(i32).reshape(1)
    routed = route(rank, request_slot, new_lengths, prefill_latent)
    incoming = exchange(routed.reshape(dp, OWN_TOK // 2, -1), both).reshape(routed.shape)

    arrays = reshard(rank, ffn_gain, w_gate, w_up, w_down, dp, tp, width, unit_pad)

    y_rank = lax.axis_index("y").astype(i32).reshape(1)
    each = w_out.shape[0] // ring
    w_turned = w_out.transpose(0, 2, 1)
    out_pieces = []
    for k in range(1, ring):
        piece = lax.dynamic_slice_in_dim(w_turned, (y_rank[0] + k) % ring * each, each, 0)
        pairs = [(j, (j + k) % ring) for j in range(ring)]
        out_pieces.append(lax.ppermute(piece, "y", pairs))

    ctx_lengths, _ = lax.optimization_barrier((ctx_lengths, arrays[0]))
    tokens = jnp.pad(step_latents.transpose(1, 0, 2), ((0, 0), (0, 16 - steps), (0, 0)))
    acc, side = attend_cache(
        ctx_lengths, queries, in_hbm(kv_cache.transpose(0, 2, 1)), tokens
    )
    my_lengths = lax.dynamic_index_in_dim(new_lengths, dp_rank, 0, keepdims=False)
    heads_out = attend_new(
        rank, my_lengths, queries, incoming, swap_cores(incoming), acc, side, w_uv, dp, ring
    )
    every = exchange(heads_out.reshape((dp,) + heads_out.shape[2:]), both).reshape(total, -1)

    def along_x(piece, k, sign):
        return lax.ppermute(piece, "tp", [(j, partner(j, tp, k, sign)) for j in range(tp)])

    pieces = {k: (arrays[n], at) for k, (n, at) in piece_places(tp).items()}
    if tp > 2:
        plus, minus = along_x(arrays[2], 2, 1), along_x(arrays[3], 2, -1)
        far, _ = lax.optimization_barrier((arrays[4:6], (plus, minus)))
        far = [along_x(far[0], 2, 1), along_x(far[1], 2, -1)]
        every, _ = lax.optimization_barrier((every, (plus, minus, far)))
    parts = project(gather_heads(y_rank, w_turned, out_pieces), every, tp)
    parts = exchange(parts.reshape((ring * tp,) + parts.shape[2:]), ("y", "tp"))
    if tp > 2:
        pieces[2], pieces[6] = (plus, 0), (minus, 0)
        swapped = [along_x(plus[1:], 1, 1), along_x(minus[1:], 1, 1)]
        far = [along_x(far[0], 2, 1), along_x(far[1], 3, -1)]
        parts, _ = lax.optimization_barrier((parts, (swapped, far)))
        pieces[3], pieces[7] = (swapped[0], 0), (swapped[1], 0)
        pieces[4], pieces[5] = (far[0], 0), (far[1], 0)
    pieces[1] = along_x(arrays[1], 1, 1), 0
    pieces = [pieces[k] for k in range(tp)]
    hidden_t = call(
        functools.partial(hidden_kernel, dp, per_owner, steps),
        jax.ShapeDtypeStruct((PAD, total), f32),
        name="turn_hidden",
    )(hidden.transpose(2, 0, 1).reshape(width, total))
    mixed, sent = make_mixed(parts, hidden_t, dp, width)
    x = exchange(sent, both)
    groups = [[k for k in range(tp) if k // 2 != 2], [k for k in range(tp) if k // 2 == 2]]
    groups = [group for group in groups if group]
    places = [(lambda array: array) if k // 2 == 2 else in_hbm for k in range(tp)]
    weights = [
        collect([pieces[k] for k in group], [places[k] for k in group], 2 * units)
        for group in groups
    ]
    keep, send = gate_up(rank, weights, groups, x)
    along = [[2 * n + core for n in range(tp // 2)] for core in range(2)]
    parts = exchange(add_cores(keep, swap_cores(send), 2 * units), "tp", along)
    parts, turned_down = lax.optimization_barrier((parts, turn(pieces, [in_hbm] * tp, 2 * units)))
    same = exchange(activate(parts, model_width, units, unit_pad), "tp", along)
    other = swap_cores(same)
    parts = exchange(down(rank, turned_down, same, other, dp, width), both)
    out = call(
        functools.partial(finish_kernel, dp, per_owner, steps),
        jax.ShapeDtypeStruct((width, steps, total // steps), bf16),
        name="finish",
    )(parts, mixed)
    return out.transpose(1, 2, 0)


def solution(mesh):
    devices = mesh.devices
    ring = 2
    devices = devices.reshape(devices.shape[0] // ring, ring, devices.shape[1])
    dp, tp = ("z", "y"), "tp"
    every = ("z", "y", "tp")
    return jax.shard_map(
        shards,
        mesh=jax.sharding.Mesh(devices, every),
        in_specs=(
            P(dp, None),
            P(),
            P(),
            P(dp),
            P(dp, None, None),
            P(None, dp, tp, None),
            P(None, dp, None),
            P(tp, None, None),
            P(tp, None, dp),
            P(None, None, every),
            P(),
            P(None, every),
            P(None, every),
            P(every, None),
        ),
        out_specs=P(None, None, every),
        check_vma=False,
    )
```

```python
import functools

import jax
import jax.numpy as jnp
from jax import lax
from jax.experimental import pallas as pl
from jax.experimental.pallas import tpu as pltpu
from jax.sharding import PartitionSpec as P

LAT = 512
QKD = 192
OWN_TOK = 16
PAD = 32
GROUP = 4

masked_score = -1e30
norm_eps = 1e-06
bf16, f32, i32 = jnp.bfloat16, jnp.float32, jnp.int32

NT = (((1,), (1,)), ((), ()))
NN = (((1,), (0,)), ((), ()))


def dot(a, b, dims=NN):
    return lax.dot_general(a, b, dims, preferred_element_type=f32)


def iota(shape, dim):
    return lax.broadcasted_iota(i32, shape, dim)


def call(body, out_shape, cost=(0, 0), mib=16, **kwargs):
    return pl.pallas_call(
        body,
        out_shape=out_shape,
        compiler_params=pltpu.CompilerParams(vmem_limit_bytes=mib * 1024 * 1024),
        cost_estimate=pl.CostEstimate(flops=cost[0], bytes_accessed=cost[1], transcendentals=0),
        **kwargs,
    )


def in_hbm(x):
    return pltpu.with_memory_space_constraint(x, pltpu.HBM)


def share_picker(tp, width, turn):
    shape = (tp * width, -(-tp // GROUP) * GROUP * PAD)
    column = iota(shape, 1)
    place = column % PAD
    slot = (column // PAD) % GROUP
    rank = column // (GROUP * PAD) * GROUP + (slot + GROUP - turn) % GROUP
    hit = (iota(shape, 0) == rank * width + place) & (place < width)
    return jnp.where(hit, 1.0, 0.0).astype(bf16)


def source_in_group(rank, slot):
    return (slot + GROUP - rank % GROUP) % GROUP


def partner(rank, tp, k, sign):
    x = (rank // 2 + sign * (k // 2) + tp // 2) % (tp // 2)
    return 2 * x + ((rank % 2) ^ (k % 2))


def token_picker(dp, per_owner, steps):
    total = dp * per_owner * steps
    shape = (total, total)
    row = iota(shape, 0)
    step, request = row // (dp * per_owner), row % (dp * per_owner)
    wanted = request * steps + step
    return jnp.where(iota(shape, 1) == wanted, 1.0, 0.0).astype(bf16)


def route_kernel(rank_ref, slot_ref, len_ref, rows_ref, out_ref):
    count = slot_ref.shape[1]
    per_owner, owners = len_ref.shape
    total = rows_ref.shape[1]
    square = (count, count)
    sub, lane = iota(square, 0), iota(square, 1)
    slot_row = slot_ref[...]
    spread = jnp.where(iota((owners, count), 1) // per_owner == iota((owners, count), 0), 1.0, 0.0)
    wide = dot(len_ref[...].astype(f32).astype(bf16), spread.astype(bf16))
    own = iota(wide.shape, 1) % per_owner == iota(wide.shape, 0)
    len_row = jnp.sum(jnp.where(own, wide, 0.0), axis=0, keepdims=True).astype(i32)
    len_col = jnp.sum(jnp.where(sub == lane, len_row, 0), axis=1, keepdims=True)
    slot_col = jnp.sum(jnp.where(sub == lane, slot_row, 0), axis=1, keepdims=True)
    hot = slot_col == lane
    hot_t = sub == slot_row
    rows_col = jnp.sum(jnp.where(hot, len_row, 0), axis=1, keepdims=True)
    rows_row = jnp.sum(jnp.where(hot_t, len_col, 0), axis=0, keepdims=True)
    owner_start = jnp.sum(jnp.where(sub < lane, len_col, 0), axis=0, keepdims=True)
    start_col = jnp.sum(jnp.where(lane < sub, rows_row, 0), axis=1, keepdims=True)
    target_col = jnp.sum(jnp.where(hot, owner_start, 0), axis=1, keepdims=True)
    at = iota((count, total), 1)
    inside = (at >= start_col) & (at < start_col + rows_col)
    shift = jnp.sum(jnp.where(inside, target_col - start_col, 0), axis=0, keepdims=True)
    target = iota((1, total), 1) + shift
    half = OWN_TOK // 2
    row = iota((total // 2, total), 0)
    wanted = row // half * OWN_TOK + rank_ref[0] % 2 * half + row % half
    pick = jnp.where(wanted == target, 1.0, 0.0).astype(bf16)
    out_ref[...] = dot(pick, rows_ref[...], NT).astype(bf16)


def route(rank, request_slot, new_lengths, prefill_latent):
    total, width = prefill_latent.shape
    return call(
        route_kernel,
        jax.ShapeDtypeStruct((total // 2, width), bf16),
        (total * total * width, 3 * total * width),
        grid=(1,),
        in_specs=[
            pl.BlockSpec(memory_space=pltpu.SMEM),
            pl.BlockSpec((1, request_slot.size), lambda c: (0, 0)),
            pl.BlockSpec(new_lengths.shape[::-1], lambda c: (0, 0)),
            pl.BlockSpec((width, total), lambda c: (0, 0)),
        ],
        out_specs=pl.BlockSpec((total // 2, width), lambda c: (0, 0)),
        name="route",
    )(rank, in_hbm(request_slot.reshape(1, -1)), in_hbm(new_lengths.T), in_hbm(prefill_latent.T))


def piece_places(tp):
    arrays = [(0,), (1,), (2, 3), (6, 7), (4,), (5,)]
    arrays = [[k for k in ks if k < tp] for ks in arrays]
    arrays = [ks for ks in arrays if ks]
    return {k: (n, at) for n, ks in enumerate(arrays) for at, k in enumerate(ks)}


def reshard_kernel(tp, width, rank_ref, gain_ref, wg_ref, wu_ref, wd_ref, *refs):
    *outs, all_scr, pick_scr, sort_scr = refs
    block = tp * width
    units = wg_ref.shape[0]
    lanes = GROUP * PAD

    @pl.when(pl.program_id(0) == 0)
    def _():
        for i in range(GROUP):
            pick_scr[i] = share_picker(tp, width, i)
        all_scr[3 * units :, :] = jnp.zeros((all_scr.shape[0] - 3 * units, all_scr.shape[1]), bf16)

    for n, w_ref in enumerate((wg_ref, wu_ref, wd_ref)):
        value = w_ref[...]
        if n < 2:
            value = (value.astype(f32) * gain_ref[...]).astype(bf16)
        all_scr[n * units : (n + 1) * units, :] = value
    slot_of = iota((all_scr.shape[0], lanes), 1) // PAD
    places = piece_places(tp)
    for u in range(outs[0].shape[1]):
        for i in range(GROUP):
            first = (u * GROUP + i) * block
            sort_scr[u, i] = dot(all_scr[:, first : first + block], pick_scr[i]).astype(bf16)
        for k in range(tp):
            target = partner(rank_ref[0], tp, k, 1)
            tile = pl.multiple_of(target // GROUP * lanes, lanes)
            value = None
            for slot in range(GROUP):
                part = sort_scr[u, source_in_group(target, slot), :, pl.ds(tile, lanes)]
                value = part if value is None else jnp.where(slot_of == slot, part, value)
            array, at = places[k]
            outs[array][at, u] = value


def reshard(rank, gain, w_gate, w_up, w_down, dp, tp, width, unit_pad):
    units = w_gate.shape[1]
    count = dp // GROUP
    each = 2 if count % 2 == 0 else 1
    block = tp * width * GROUP * each
    lanes = GROUP * PAD
    rows = 2 * units + unit_pad
    w_spec = pl.BlockSpec((units, block), lambda c: (0, c))
    tiles = -(-tp // GROUP)
    places = piece_places(tp)
    owners = [n for n, _ in places.values()]
    sizes = [owners.count(n) for n in range(max(owners) + 1)]
    return call(
        functools.partial(reshard_kernel, tp, width),
        tuple(pltpu.HBM((size, count, rows, lanes), bf16) for size in sizes),
        (2 * 3 * dp * tp * PAD * tp * width * units, 14 * w_gate.size),
        grid=(count // each,),
        in_specs=[
            pl.BlockSpec(memory_space=pltpu.SMEM),
            pl.BlockSpec((1, block), lambda c: (0, c)),
            w_spec,
            w_spec,
            w_spec,
        ],
        out_specs=tuple(
            pl.BlockSpec((size, each, rows, lanes), lambda c: (0, c, 0, 0)) for size in sizes
        ),
        scratch_shapes=[
            pltpu.VMEM((rows, block), bf16),
            pltpu.VMEM((GROUP, tp * width, tiles * lanes), bf16),
            pltpu.VMEM((each, GROUP, rows, tiles * lanes), bf16),
        ],
        name="reshard",
        mib=24,
    )(rank, in_hbm(gain.reshape(1, -1)), in_hbm(w_gate.T), in_hbm(w_up.T), in_hbm(w_down))


def turn_kernel(first, *refs):
    _, count, _, lanes = refs[0].shape
    eye = jnp.where(iota((lanes, lanes), 0) == iota((lanes, lanes), 1), 1.0, 0.0).astype(bf16)
    for c in range(count):
        x = jnp.concatenate([ref[0, c, first:, :] for ref in refs[:-1]], axis=0)
        refs[-1][c * lanes : (c + 1) * lanes, :] = dot(eye, x, NT).astype(bf16)


def turn(pieces, places, first):
    _, count, rows, lanes = pieces[0][0].shape
    depth = len(pieces) * (rows - first)
    each = 4 if count % 4 == 0 else 1
    return call(
        functools.partial(turn_kernel, first),
        jax.ShapeDtypeStruct((count * lanes, depth), bf16),
        (2 * lanes * lanes * depth * count, 4 * depth * lanes * count),
        grid=(count // each,),
        in_specs=[
            pl.BlockSpec((1, each, rows, lanes), lambda c, at=at: (at, c, 0, 0)) for _, at in pieces
        ],
        out_specs=pl.BlockSpec((each * lanes, depth), lambda c: (c, 0)),
        name="turn",
    )(*[place(array) for (array, _), place in zip(pieces, places)])


def hidden_kernel(dp, per_owner, steps, h_ref, out_ref):
    width = h_ref.shape[0]
    eye = jnp.where(iota((PAD, width), 0) == iota((PAD, width), 1), 1.0, 0.0).astype(bf16)
    placed = dot(h_ref[...], token_picker(dp, per_owner, steps)).astype(bf16)
    out_ref[...] = dot(eye, placed)


def cache_kernel(ctx_ref, q_ref, kv_ref, tok_ref, acc_ref, side_ref):
    at = pl.program_id(0)
    scale = QKD ** (-0.5)
    steps, _, heads, width = q_ref.shape
    rows = steps * heads
    query = q_ref[...].reshape(rows, width)
    keys = kv_ref[0]
    toks = tok_ref[0]
    scores = dot(query, keys) * scale
    scores = jnp.where(iota(scores.shape, 1) < ctx_ref[at], scores, masked_score)
    fresh = dot(query, toks, NT) * scale
    step = iota(fresh.shape, 0) // heads
    fresh = jnp.where(iota(fresh.shape, 1) <= step, fresh, masked_score)
    top = jnp.maximum(
        jnp.max(scores, axis=1, keepdims=True), jnp.max(fresh, axis=1, keepdims=True)
    )
    scores = jnp.exp(scores - top)
    fresh = jnp.exp(fresh - top)
    total = jnp.sum(scores, axis=1, keepdims=True) + jnp.sum(fresh, axis=1, keepdims=True)
    acc_ref[0] = dot(scores.astype(bf16), keys[:LAT], NT) + dot(fresh.astype(bf16), toks[:, :LAT])
    side_ref[0] = jnp.where(iota(side_ref.shape[1:], 1) == 0, top, total)


def attend_cache(ctx_lengths, queries, kv_cache, tokens):
    steps, per_owner, heads, width = queries.shape
    keys = kv_cache.shape[2]
    rows = steps * heads
    side_spec = pl.BlockSpec((1, rows, 128), lambda q: (q, 0, 0))
    return call(
        cache_kernel,
        (pltpu.HBM((per_owner, rows, LAT), f32), pltpu.HBM((per_owner, rows, 128), f32)),
        (2 * per_owner * rows * keys * (width + LAT), 2 * kv_cache.size),
        grid=(per_owner,),
        in_specs=[
            pl.BlockSpec(memory_space=pltpu.SMEM),
            pl.BlockSpec((steps, 1, heads, width), lambda q: (0, q, 0, 0)),
            pl.BlockSpec((1, width, keys), lambda q: (q, 0, 0)),
            pl.BlockSpec((1, tokens.shape[1], width), lambda q: (q, 0, 0)),
        ],
        out_specs=(pl.BlockSpec((1, rows, LAT), lambda q: (q, 0, 0)), side_spec),
        name="attend_cache",
    )(ctx_lengths, queries, kv_cache, tokens)


def merge_kernel(rank_ref, len_ref, q_ref, new_ref, other_ref, acc_ref, side_ref, uv_ref, out_ref):
    scale = QKD ** (-0.5)
    steps, per_owner, heads, width = q_ref.shape
    rows = steps * heads
    new = jnp.concatenate([new_ref[...], other_ref[...]], axis=0)
    query = jnp.concatenate([q_ref[:, q].reshape(rows, width) for q in range(per_owner)], axis=0)
    scores = dot(query, new, NT) * scale
    half = OWN_TOK // 2
    column = iota(scores.shape, 1)
    core = jnp.where(column < scores.shape[1] // 2, rank_ref[0] % 2, 1 - rank_ref[0] % 2)
    place = core * half + column % half
    owner_row = iota(scores.shape, 0) // rows
    first = jnp.zeros(scores.shape, i32)
    last = jnp.zeros(scores.shape, i32)
    start = jnp.int32(0)
    for q in range(per_owner):
        end = start + len_ref[q]
        first = jnp.where(owner_row == q, start, first)
        last = jnp.where(owner_row == q, end, last)
        start = end
    scores = jnp.where((place >= first) & (place < last), scores, masked_score)
    total_rows = per_owner * rows
    side = side_ref[...].reshape(total_rows, 128)
    old_top, old_sum = side[:, :1], side[:, 1:2]
    top = jnp.maximum(jnp.max(scores, axis=1, keepdims=True), old_top)
    scores = jnp.exp(scores - top)
    weight = jnp.exp(old_top - top)
    total = jnp.sum(scores, axis=1, keepdims=True) + old_sum * weight
    acc = acc_ref[...].reshape(total_rows, LAT) * weight + dot(scores.astype(bf16), new[:, :LAT])
    latent = (acc / total).astype(bf16)
    values = uv_ref.shape[2]
    groups = per_owner * steps
    each = out_ref.shape[3] // values
    for h in range(0, heads, 2):
        full = dot(latent, jnp.concatenate([uv_ref[h], uv_ref[h + 1]], axis=1))
        full = full.reshape(groups, heads, 2 * values)
        wanted = h + iota(full.shape, 2) // values
        mine = jnp.sum(jnp.where(iota(full.shape, 1) == wanted, full, 0.0), axis=1).astype(bf16)
        place = (h % each) * values
        out_ref[:, h // each, :, place : place + 2 * values] = jnp.broadcast_to(
            mine[None], (out_ref.shape[0], groups, 2 * values)
        )


def attend_new(rank, my_lengths, queries, new_rows, other_rows, acc, side, w_uv, dp, parts):
    steps, per_owner, heads, _ = queries.shape
    whole = pl.BlockSpec(memory_space=pltpu.VMEM)
    return call(
        merge_kernel,
        jax.ShapeDtypeStruct(
            (dp // parts, parts, per_owner * steps, heads // parts * w_uv.shape[2]), bf16
        ),
        (8 * new_rows.size * per_owner * steps * heads, 2 * w_uv.size),
        grid=(1,),
        in_specs=[
            pl.BlockSpec(memory_space=pltpu.SMEM),
            pl.BlockSpec(memory_space=pltpu.SMEM),
            whole,
            whole,
            whole,
            pl.BlockSpec(acc.shape, lambda c: (0, 0, 0)),
            pl.BlockSpec(side.shape, lambda c: (0, 0, 0)),
            whole,
        ],
        out_specs=whole,
        name="attend_new",
    )(rank, my_lengths, queries, new_rows, other_rows, in_hbm(acc), in_hbm(side), w_uv)


def own_heads_kernel(rank_ref, w_ref, out_ref):
    heads, _, values = w_ref.shape
    for h in range(heads):
        out_ref[:, h * values : (h + 1) * values] = w_ref[h]


def own_heads(rank, own, ring):
    total, features, values = own.shape
    heads = total // ring
    return call(
        own_heads_kernel,
        jax.ShapeDtypeStruct((features, heads * values), bf16),
        (0, 4 * heads * features * values),
        grid_spec=pltpu.PrefetchScalarGridSpec(
            num_scalar_prefetch=1,
            grid=(1,),
            in_specs=[pl.BlockSpec((heads, features, values), lambda c, rank: (rank[0], 0, 0))],
            out_specs=pl.BlockSpec(memory_space=pltpu.VMEM),
        ),
        name="own_heads",
    )(rank, in_hbm(own))


def project_kernel(rank_ref, x_ref, own_ref, *refs):
    *w_refs, out_ref = refs
    ring, tp = out_ref.shape[:2]
    x = x_ref[...].T
    for k in range(ring):
        if k == 0:
            weights = own_ref[...]
        else:
            w_ref = w_refs[k - 1]
            weights = jnp.concatenate([w_ref[h] for h in range(w_ref.shape[0])], axis=1)
        width = weights.shape[0] // tp
        target = (rank_ref[0] + ring - k) % ring
        value = dot(weights, x)
        spare = jnp.zeros((PAD - width, value.shape[1]), f32)
        for j in range(tp):
            part = jnp.concatenate([value[j * width : (j + 1) * width], spare], axis=0)
            out_ref[target, j] = part.astype(bf16)


def project(rank, own, pieces, every, tp):
    ring, columns = 1 + len(pieces), every.shape[0]
    whole = pl.BlockSpec(memory_space=pltpu.VMEM)
    return call(
        project_kernel,
        jax.ShapeDtypeStruct((ring, tp, PAD, columns), bf16),
        (2 * ring * own.size * columns, 2 * (ring * own.size + every.size)),
        in_specs=[pl.BlockSpec(memory_space=pltpu.SMEM)] + [whole] * (1 + ring),
        out_specs=whole,
        name="project",
    )(rank, every, own, *pieces)


def split_sum(value):
    high = value.astype(bf16).astype(f32)
    return high, value - high


def stack_halves(value, width):
    half = value.shape[1] // 2
    return jnp.concatenate([value[:width, :half], value[:width, half:]], axis=0)


def mixed_kernel(width, part_ref, hidden_ref, mixed_ref, out_ref):
    mixed = jnp.sum(part_ref[...].astype(f32), axis=0) + hidden_ref[...]
    mixed_ref[...] = mixed
    sent = stack_halves(mixed, width).astype(bf16)
    out_ref[...] = jnp.broadcast_to(sent[None], out_ref.shape)


def make_mixed(parts, hidden_t, dp, width):
    _, rows, columns = parts.shape
    return call(
        functools.partial(mixed_kernel, width),
        (
            jax.ShapeDtypeStruct((rows, columns), f32),
            jax.ShapeDtypeStruct((dp, 2 * width, columns // 2), bf16),
        ),
        (parts.size, 4 * parts.size),
        name="make_mixed",
    )(parts, hidden_t)


def gate_kernel(groups, rank_ref, x_ref, *refs):
    *w_refs, keep_ref, send_ref = refs
    units = w_refs[0].shape[1]
    width = x_ref.shape[1] // 2
    blocks = []
    for c in range(0, x_ref.shape[0], GROUP):
        for slot in range(GROUP):
            piece = x_ref[c + source_in_group(rank_ref[0], slot)].astype(f32)
            spare = jnp.zeros((PAD - width, piece.shape[1]), f32)
            right = jnp.concatenate([piece[width:], spare], axis=0)
            blocks.append(jnp.concatenate([piece[:PAD], right], axis=1))
    x = jnp.concatenate(blocks, axis=0)
    squares = jnp.where(iota(x.shape, 0) % PAD < width, x * x, 0.0)
    high, low = split_sum(jnp.sum(squares, axis=0, keepdims=True))
    row = iota((16, x.shape[1]), 0)
    tail = jnp.where(row == 0, high, jnp.where(row == 1, low, 0.0)).astype(bf16)
    x = x.astype(bf16)
    for w_ref, group in zip(w_refs, groups):
        for at, k in enumerate(group):
            n = partner(rank_ref[0], 2 * keep_ref.shape[0], k, -1) // 2
            out_ref = send_ref if k % 2 else keep_ref
            out_ref[n, :units, :] = dot(w_ref[at], x).astype(bf16)
            out_ref[n, units:, :] = tail


def collect_kernel(*refs):
    for n, w_ref in enumerate(refs[:-1]):
        lanes = w_ref.shape[3]
        for c in range(w_ref.shape[1]):
            refs[-1][n, :, c * lanes : (c + 1) * lanes] = w_ref[0, c]


def collect(pieces, places, units):
    tp = len(pieces)
    _, count, _, lanes = pieces[0][0].shape
    out_shape = (tp, units, count * lanes)
    return call(
        collect_kernel,
        jax.ShapeDtypeStruct(out_shape, bf16),
        (0, 4 * tp * units * count * lanes),
        grid=(1,),
        in_specs=[
            pl.BlockSpec((1, count, units, lanes), lambda c, at=at: (at, 0, 0, 0)) for _, at in pieces
        ],
        out_specs=pl.BlockSpec(memory_space=pltpu.VMEM),
        name="collect",
    )(*[place(array) for (array, _), place in zip(pieces, places)])


def gate_up(rank, weights, groups, x):
    tp = sum(len(group) for group in groups)
    _, units, depth = weights[0].shape
    size = tp * units * depth
    columns = 2 * x.shape[2]
    whole = pl.BlockSpec(memory_space=pltpu.VMEM)
    out = jax.ShapeDtypeStruct((tp // 2, units + 16, columns), bf16)
    return call(
        functools.partial(gate_kernel, groups),
        (out, out),
        (2 * size * columns, 2 * size + 2 * x.size),
        in_specs=[pl.BlockSpec(memory_space=pltpu.SMEM)] + [whole] * (1 + len(weights)),
        out_specs=(whole, whole),
        name="gate_up",
    )(rank, x, *weights)


def add_kernel(units, a_ref, b_ref, out_ref):
    out_ref[:, :units, :] = (
        a_ref[:, :units, :].astype(f32) + b_ref[:, :units, :].astype(f32)
    ).astype(bf16)
    tail = a_ref[:, units:, :].astype(f32) + b_ref[:, units:, :].astype(f32)
    high, low = split_sum(tail[:, 0:1] + tail[:, 1:2])
    row = iota(tail.shape, 1)
    tail = jnp.where(row == 0, high, jnp.where(row == 1, low, 0.0))
    out_ref[:, units:, :] = tail.astype(bf16)


def add_cores(a, b, units):
    return call(
        functools.partial(add_kernel, units),
        jax.ShapeDtypeStruct(a.shape, bf16),
        (2 * a.size, 6 * a.size),
        name="add_cores",
    )(a, b)


def activate_kernel(model_width, units, part_ref, out_ref):
    sums = jnp.sum(part_ref[...].astype(f32), axis=0)
    squares = sums[2 * units : 2 * units + 1] + sums[2 * units + 1 : 2 * units + 2]
    factor = lax.rsqrt(squares / model_width + norm_eps)
    gate = sums[:units] * factor
    up = sums[units : 2 * units] * factor
    value = gate / (1.0 + jnp.exp(-gate)) * up
    spare = out_ref.shape[1] - units
    if spare:
        value = jnp.concatenate([value, jnp.zeros((spare, value.shape[1]), f32)], axis=0)
    out_ref[...] = jnp.broadcast_to(value.astype(bf16)[None], out_ref.shape)


def activate(parts, model_width, units, unit_pad):
    tp, _, columns = parts.shape
    return call(
        functools.partial(activate_kernel, model_width, units),
        jax.ShapeDtypeStruct((tp, unit_pad, columns), bf16),
        (10 * parts.size, 4 * parts.size),
        name="activate",
    )(parts)


def down_kernel(rank_ref, w_ref, same_ref, other_ref, out_ref):
    tp = 2 * same_ref.shape[0]
    refs = (same_ref, other_ref)
    sources = [partner(rank_ref[0], tp, k, -1) // 2 for k in range(tp)]
    x = jnp.concatenate([refs[k % 2][n] for k, n in enumerate(sources)], axis=0)
    value = dot(w_ref[...], x)
    count, rows, _ = out_ref.shape
    value = value.reshape(count, PAD, value.shape[1])
    for n in range(count):
        first, slot = n // GROUP * GROUP, n % GROUP
        out_ref[first + source_in_group(rank_ref[0], slot)] = stack_halves(
            value[n], rows // 2
        ).astype(bf16)


def down(rank, turned, same, other, dp, width):
    rows, depth = turned.shape
    columns = same.shape[2]
    block = 256 if rows % 256 == 0 else 128
    x_spec = pl.BlockSpec(same.shape, lambda c: (0, 0, 0))
    return call(
        down_kernel,
        jax.ShapeDtypeStruct((dp, 2 * width, columns // 2), bf16),
        (2 * turned.size * columns, 2 * turned.size + 4 * same.size),
        grid=(rows // block,),
        in_specs=[
            pl.BlockSpec(memory_space=pltpu.SMEM),
            pl.BlockSpec((block, depth), lambda c: (c, 0)),
            x_spec,
            x_spec,
        ],
        out_specs=pl.BlockSpec((block // PAD, 2 * width, columns // 2), lambda c: (c, 0, 0)),
        name="down",
    )(rank, turned, same, other)


def finish_kernel(dp, per_owner, steps, part_ref, mixed_ref, out_ref):
    value = jnp.sum(part_ref[...].astype(f32), axis=0)
    width = value.shape[0] // 2
    value = jnp.concatenate([value[:width], value[width:]], axis=1) + mixed_ref[:width]
    picked = dot(value.astype(bf16), token_picker(dp, per_owner, steps), NT)
    picked = picked.astype(bf16)
    each = out_ref.shape[2]
    for s in range(steps):
        out_ref[:, s, :] = picked[:, s * each : (s + 1) * each]


def exchange(x, axis, groups=None):
    return lax.all_to_all(
        x, axis, split_axis=0, concat_axis=0, tiled=True, axis_index_groups=groups
    )


def swap_cores(x):
    return lax.ppermute(x, "tp", [(j, j ^ 1) for j in range(lax.axis_size("tp"))])


def shards(
    prefill_latent,
    request_slot,
    new_lengths,
    ctx_lengths,
    kv_cache,
    queries,
    step_latents,
    w_uv,
    w_out,
    hidden,
    ffn_gain,
    w_gate,
    w_up,
    w_down,
):
    both = ("z", "y")
    ring = lax.axis_size("y")
    dp, tp = lax.axis_size("z") * ring, lax.axis_size("tp")
    dp_rank, tp_rank = lax.axis_index(both), lax.axis_index("tp")
    steps, per_owner = queries.shape[:2]
    width = hidden.shape[2]
    model_width = width * dp * tp
    units = w_gate.shape[1]
    unit_pad = -(-units // 16) * 16
    total = hidden.shape[0] * hidden.shape[1]

    rank = tp_rank.astype(i32).reshape(1)
    routed = route(rank, request_slot, new_lengths, prefill_latent)
    incoming = exchange(routed.reshape(dp, OWN_TOK // 2, -1), both).reshape(routed.shape)

    arrays = reshard(rank, ffn_gain, w_gate, w_up, w_down, dp, tp, width, unit_pad)

    y_rank = lax.axis_index("y").astype(i32).reshape(1)
    each = w_out.shape[0] // ring
    w_turned = w_out.transpose(0, 2, 1)
    out_pieces = []
    for k in range(1, ring):
        piece = lax.dynamic_slice_in_dim(w_turned, (y_rank[0] + k) % ring * each, each, 0)
        pairs = [(j, (j + k) % ring) for j in range(ring)]
        out_pieces.append(lax.ppermute(piece, "y", pairs))

    ctx_lengths, _ = lax.optimization_barrier((ctx_lengths, arrays[0]))
    tokens = jnp.pad(step_latents.transpose(1, 0, 2), ((0, 0), (0, 16 - steps), (0, 0)))
    acc, side = attend_cache(
        ctx_lengths, queries, in_hbm(kv_cache.transpose(0, 2, 1)), tokens
    )
    my_lengths = lax.dynamic_index_in_dim(new_lengths, dp_rank, 0, keepdims=False)
    heads_out = attend_new(
        rank, my_lengths, queries, incoming, swap_cores(incoming), acc, side, w_uv, dp, ring
    )
    every = exchange(heads_out.reshape((dp,) + heads_out.shape[2:]), both).reshape(total, -1)

    def along_x(piece, k, sign):
        return lax.ppermute(piece, "tp", [(j, partner(j, tp, k, sign)) for j in range(tp)])

    pieces = {k: (arrays[n], at) for k, (n, at) in piece_places(tp).items()}
    if tp > 2:
        plus, minus = along_x(arrays[2], 2, 1), along_x(arrays[3], 2, -1)
        far, _ = lax.optimization_barrier((arrays[4:6], (plus, minus)))
        far = [along_x(far[0], 2, 1), along_x(far[1], 2, -1)]
        every, _ = lax.optimization_barrier((every, (plus, minus, far)))
    parts = project(y_rank, own_heads(y_rank, w_turned, ring), out_pieces, every, tp)
    parts = exchange(parts.reshape((ring * tp,) + parts.shape[2:]), ("y", "tp"))
    if tp > 2:
        pieces[2], pieces[6] = (plus, 0), (minus, 0)
        swapped = [along_x(plus[1:], 1, 1), along_x(minus[1:], 1, 1)]
        far = [along_x(far[0], 2, 1), along_x(far[1], 3, -1)]
        parts, _ = lax.optimization_barrier((parts, far))
        pieces[3], pieces[7] = (swapped[0], 0), (swapped[1], 0)
        pieces[4], pieces[5] = (far[0], 0), (far[1], 0)
    pieces[1] = along_x(arrays[1], 1, 1), 0
    pieces = [pieces[k] for k in range(tp)]
    hidden_t = call(
        functools.partial(hidden_kernel, dp, per_owner, steps),
        jax.ShapeDtypeStruct((PAD, total), f32),
        name="turn_hidden",
    )(hidden.transpose(2, 0, 1).reshape(width, total))
    mixed, sent = make_mixed(parts, hidden_t, dp, width)
    x = exchange(sent, both)
    groups = [[k for k in range(tp) if k // 2 != 2], [k for k in range(tp) if k // 2 == 2]]
    groups = [group for group in groups if group]
    places = [(lambda array: array) if k // 2 == 2 else in_hbm for k in range(tp)]
    weights = [
        collect([pieces[k] for k in group], [places[k] for k in group], 2 * units)
        for group in groups
    ]
    keep, send = gate_up(rank, weights, groups, x)
    along = [[2 * n + core for n in range(tp // 2)] for core in range(2)]
    parts = exchange(add_cores(keep, swap_cores(send), 2 * units), "tp", along)
    parts, turned_down = lax.optimization_barrier((parts, turn(pieces, [in_hbm] * tp, 2 * units)))
    same = exchange(activate(parts, model_width, units, unit_pad), "tp", along)
    other = swap_cores(same)
    parts = exchange(down(rank, turned_down, same, other, dp, width), both)
    out = call(
        functools.partial(finish_kernel, dp, per_owner, steps),
        jax.ShapeDtypeStruct((width, steps, total // steps), bf16),
        name="finish",
    )(parts, mixed)
    return out.transpose(1, 2, 0)


def solution(mesh):
    devices = mesh.devices
    ring = 2
    devices = devices.reshape(devices.shape[0] // ring, ring, devices.shape[1])
    dp, tp = ("z", "y"), "tp"
    every = ("z", "y", "tp")
    return jax.shard_map(
        shards,
        mesh=jax.sharding.Mesh(devices, every),
        in_specs=(
            P(dp, None),
            P(),
            P(),
            P(dp),
            P(dp, None, None),
            P(None, dp, tp, None),
            P(None, dp, None),
            P(tp, None, None),
            P(tp, None, dp),
            P(None, None, every),
            P(),
            P(None, every),
            P(None, every),
            P(every, None),
        ),
        out_specs=P(None, None, every),
        check_vma=False,
    )
```

```python
import functools

import jax
import jax.numpy as jnp
from jax import lax
from jax.experimental import pallas as pl
from jax.experimental.pallas import tpu as pltpu
from jax.sharding import PartitionSpec as P

LAT = 512
QKD = 192
OWN_TOK = 16
PAD = 32
GROUP = 4

masked_score = -1e30
norm_eps = 1e-06
bf16, f32, i32 = jnp.bfloat16, jnp.float32, jnp.int32

NT = (((1,), (1,)), ((), ()))
NN = (((1,), (0,)), ((), ()))


def dot(a, b, dims=NN):
    return lax.dot_general(a, b, dims, preferred_element_type=f32)


def iota(shape, dim):
    return lax.broadcasted_iota(i32, shape, dim)


def call(body, out_shape, cost=(0, 0), mib=16, **kwargs):
    return pl.pallas_call(
        body,
        out_shape=out_shape,
        compiler_params=pltpu.CompilerParams(vmem_limit_bytes=mib * 1024 * 1024),
        cost_estimate=pl.CostEstimate(flops=cost[0], bytes_accessed=cost[1], transcendentals=0),
        **kwargs,
    )


def in_hbm(x):
    return pltpu.with_memory_space_constraint(x, pltpu.HBM)


def share_picker(tp, width, turn):
    shape = (tp * width, -(-tp // GROUP) * GROUP * PAD)
    column = iota(shape, 1)
    place = column % PAD
    slot = (column // PAD) % GROUP
    rank = column // (GROUP * PAD) * GROUP + (slot + GROUP - turn) % GROUP
    hit = (iota(shape, 0) == rank * width + place) & (place < width)
    return jnp.where(hit, 1.0, 0.0).astype(bf16)


def source_in_group(rank, slot):
    return (slot + GROUP - rank % GROUP) % GROUP


def partner(rank, tp, k, sign):
    x = (rank // 2 + sign * (k // 2) + tp // 2) % (tp // 2)
    return 2 * x + ((rank % 2) ^ (k % 2))


def token_picker(dp, per_owner, steps):
    total = dp * per_owner * steps
    shape = (total, total)
    row = iota(shape, 0)
    step, request = row // (dp * per_owner), row % (dp * per_owner)
    wanted = request * steps + step
    return jnp.where(iota(shape, 1) == wanted, 1.0, 0.0).astype(bf16)


def route_kernel(rank_ref, slot_ref, len_ref, rows_ref, out_ref):
    count = slot_ref.shape[1]
    per_owner, owners = len_ref.shape
    total = rows_ref.shape[1]
    square = (count, count)
    sub, lane = iota(square, 0), iota(square, 1)
    slot_row = slot_ref[...]
    spread = jnp.where(iota((owners, count), 1) // per_owner == iota((owners, count), 0), 1.0, 0.0)
    wide = dot(len_ref[...].astype(f32).astype(bf16), spread.astype(bf16))
    own = iota(wide.shape, 1) % per_owner == iota(wide.shape, 0)
    len_row = jnp.sum(jnp.where(own, wide, 0.0), axis=0, keepdims=True).astype(i32)
    len_col = jnp.sum(jnp.where(sub == lane, len_row, 0), axis=1, keepdims=True)
    slot_col = jnp.sum(jnp.where(sub == lane, slot_row, 0), axis=1, keepdims=True)
    hot = slot_col == lane
    hot_t = sub == slot_row
    rows_col = jnp.sum(jnp.where(hot, len_row, 0), axis=1, keepdims=True)
    rows_row = jnp.sum(jnp.where(hot_t, len_col, 0), axis=0, keepdims=True)
    owner_start = jnp.sum(jnp.where(sub < lane, len_col, 0), axis=0, keepdims=True)
    start_col = jnp.sum(jnp.where(lane < sub, rows_row, 0), axis=1, keepdims=True)
    target_col = jnp.sum(jnp.where(hot, owner_start, 0), axis=1, keepdims=True)
    at = iota((count, total), 1)
    inside = (at >= start_col) & (at < start_col + rows_col)
    shift = jnp.sum(jnp.where(inside, target_col - start_col, 0), axis=0, keepdims=True)
    target = iota((1, total), 1) + shift
    half = OWN_TOK // 2
    row = iota((total // 2, total), 0)
    wanted = row // half * OWN_TOK + rank_ref[0] % 2 * half + row % half
    pick = jnp.where(wanted == target, 1.0, 0.0).astype(bf16)
    out_ref[...] = dot(pick, rows_ref[...], NT).astype(bf16)


def route(rank, request_slot, new_lengths, prefill_latent):
    total, width = prefill_latent.shape
    return call(
        route_kernel,
        jax.ShapeDtypeStruct((total // 2, width), bf16),
        (total * total * width, 3 * total * width),
        grid=(1,),
        in_specs=[
            pl.BlockSpec(memory_space=pltpu.SMEM),
            pl.BlockSpec((1, request_slot.size), lambda c: (0, 0)),
            pl.BlockSpec(new_lengths.shape[::-1], lambda c: (0, 0)),
            pl.BlockSpec((width, total), lambda c: (0, 0)),
        ],
        out_specs=pl.BlockSpec((total // 2, width), lambda c: (0, 0)),
        name="route",
    )(rank, in_hbm(request_slot.reshape(1, -1)), in_hbm(new_lengths.T), in_hbm(prefill_latent.T))


def piece_places(tp):
    arrays = [(0,), (1,), (2, 3), (6, 7), (4,), (5,)]
    arrays = [[k for k in ks if k < tp] for ks in arrays]
    arrays = [ks for ks in arrays if ks]
    return {k: (n, at) for n, ks in enumerate(arrays) for at, k in enumerate(ks)}


def reshard_kernel(tp, width, rank_ref, gain_ref, wg_ref, wu_ref, wd_ref, *refs):
    *outs, all_scr, pick_scr, sort_scr = refs
    block = tp * width
    units = wg_ref.shape[0]
    lanes = GROUP * PAD

    @pl.when(pl.program_id(0) == 0)
    def _():
        for i in range(GROUP):
            pick_scr[i] = share_picker(tp, width, i)
        all_scr[3 * units :, :] = jnp.zeros((all_scr.shape[0] - 3 * units, all_scr.shape[1]), bf16)

    for n, w_ref in enumerate((wg_ref, wu_ref, wd_ref)):
        value = w_ref[...]
        if n < 2:
            value = (value.astype(f32) * gain_ref[...]).astype(bf16)
        all_scr[n * units : (n + 1) * units, :] = value
    slot_of = iota((all_scr.shape[0], lanes), 1) // PAD
    places = piece_places(tp)
    for u in range(outs[0].shape[1]):
        for i in range(GROUP):
            first = (u * GROUP + i) * block
            sort_scr[u, i] = dot(all_scr[:, first : first + block], pick_scr[i]).astype(bf16)
        for k in range(tp):
            target = partner(rank_ref[0], tp, k, 1)
            tile = pl.multiple_of(target // GROUP * lanes, lanes)
            value = None
            for slot in range(GROUP):
                part = sort_scr[u, source_in_group(target, slot), :, pl.ds(tile, lanes)]
                value = part if value is None else jnp.where(slot_of == slot, part, value)
            array, at = places[k]
            outs[array][at, u] = value


def reshard(rank, gain, w_gate, w_up, w_down, dp, tp, width, unit_pad):
    units = w_gate.shape[1]
    count = dp // GROUP
    each = 2 if count % 2 == 0 else 1
    block = tp * width * GROUP * each
    lanes = GROUP * PAD
    rows = 2 * units + unit_pad
    w_spec = pl.BlockSpec((units, block), lambda c: (0, c))
    tiles = -(-tp // GROUP)
    places = piece_places(tp)
    owners = [n for n, _ in places.values()]
    sizes = [owners.count(n) for n in range(max(owners) + 1)]
    return call(
        functools.partial(reshard_kernel, tp, width),
        tuple(pltpu.HBM((size, count, rows, lanes), bf16) for size in sizes),
        (2 * 3 * dp * tp * PAD * tp * width * units, 14 * w_gate.size),
        grid=(count // each,),
        in_specs=[
            pl.BlockSpec(memory_space=pltpu.SMEM),
            pl.BlockSpec((1, block), lambda c: (0, c)),
            w_spec,
            w_spec,
            w_spec,
        ],
        out_specs=tuple(
            pl.BlockSpec((size, each, rows, lanes), lambda c: (0, c, 0, 0)) for size in sizes
        ),
        scratch_shapes=[
            pltpu.VMEM((rows, block), bf16),
            pltpu.VMEM((GROUP, tp * width, tiles * lanes), bf16),
            pltpu.VMEM((each, GROUP, rows, tiles * lanes), bf16),
        ],
        name="reshard",
        mib=24,
    )(rank, in_hbm(gain.reshape(1, -1)), in_hbm(w_gate.T), in_hbm(w_up.T), in_hbm(w_down))


def turn_kernel(first, *refs):
    _, count, _, lanes = refs[0].shape
    eye = jnp.where(iota((lanes, lanes), 0) == iota((lanes, lanes), 1), 1.0, 0.0).astype(bf16)
    for c in range(count):
        x = jnp.concatenate([ref[0, c, first:, :] for ref in refs[:-1]], axis=0)
        refs[-1][c * lanes : (c + 1) * lanes, :] = dot(eye, x, NT).astype(bf16)


def turn(pieces, places, first):
    _, count, rows, lanes = pieces[0][0].shape
    depth = len(pieces) * (rows - first)
    each = 4 if count % 4 == 0 else 1
    return call(
        functools.partial(turn_kernel, first),
        jax.ShapeDtypeStruct((count * lanes, depth), bf16),
        (2 * lanes * lanes * depth * count, 4 * depth * lanes * count),
        grid=(count // each,),
        in_specs=[
            pl.BlockSpec((1, each, rows, lanes), lambda c, at=at: (at, c, 0, 0)) for _, at in pieces
        ],
        out_specs=pl.BlockSpec((each * lanes, depth), lambda c: (c, 0)),
        name="turn",
    )(*[place(array) for (array, _), place in zip(pieces, places)])


def hidden_kernel(dp, per_owner, steps, h_ref, out_ref):
    width = h_ref.shape[0]
    eye = jnp.where(iota((PAD, width), 0) == iota((PAD, width), 1), 1.0, 0.0).astype(bf16)
    placed = dot(h_ref[...], token_picker(dp, per_owner, steps)).astype(bf16)
    out_ref[...] = dot(eye, placed)


def cache_kernel(ctx_ref, q_ref, kv_ref, tok_ref, acc_ref, side_ref):
    at = pl.program_id(0)
    scale = QKD ** (-0.5)
    steps, _, heads, width = q_ref.shape
    rows = steps * heads
    query = q_ref[...].reshape(rows, width)
    keys = kv_ref[0]
    toks = tok_ref[0]
    scores = dot(query, keys) * scale
    scores = jnp.where(iota(scores.shape, 1) < ctx_ref[at], scores, masked_score)
    fresh = dot(query, toks, NT) * scale
    step = iota(fresh.shape, 0) // heads
    fresh = jnp.where(iota(fresh.shape, 1) <= step, fresh, masked_score)
    top = jnp.maximum(
        jnp.max(scores, axis=1, keepdims=True), jnp.max(fresh, axis=1, keepdims=True)
    )
    scores = jnp.exp(scores - top)
    fresh = jnp.exp(fresh - top)
    total = jnp.sum(scores, axis=1, keepdims=True) + jnp.sum(fresh, axis=1, keepdims=True)
    acc_ref[0] = dot(scores.astype(bf16), keys[:LAT], NT) + dot(fresh.astype(bf16), toks[:, :LAT])
    side_ref[0] = jnp.where(iota(side_ref.shape[1:], 1) == 0, top, total)


def attend_cache(ctx_lengths, queries, kv_cache, tokens):
    steps, per_owner, heads, width = queries.shape
    keys = kv_cache.shape[2]
    rows = steps * heads
    side_spec = pl.BlockSpec((1, rows, 128), lambda q: (q, 0, 0))
    return call(
        cache_kernel,
        (pltpu.HBM((per_owner, rows, LAT), f32), pltpu.HBM((per_owner, rows, 128), f32)),
        (2 * per_owner * rows * keys * (width + LAT), 2 * kv_cache.size),
        grid=(per_owner,),
        in_specs=[
            pl.BlockSpec(memory_space=pltpu.SMEM),
            pl.BlockSpec((steps, 1, heads, width), lambda q: (0, q, 0, 0)),
            pl.BlockSpec((1, width, keys), lambda q: (q, 0, 0)),
            pl.BlockSpec((1, tokens.shape[1], width), lambda q: (q, 0, 0)),
        ],
        out_specs=(pl.BlockSpec((1, rows, LAT), lambda q: (q, 0, 0)), side_spec),
        name="attend_cache",
    )(ctx_lengths, queries, kv_cache, tokens)


def merge_kernel(rank_ref, len_ref, q_ref, new_ref, other_ref, acc_ref, side_ref, uv_ref, out_ref):
    scale = QKD ** (-0.5)
    steps, per_owner, heads, width = q_ref.shape
    rows = steps * heads
    new = jnp.concatenate([new_ref[...], other_ref[...]], axis=0)
    query = jnp.concatenate([q_ref[:, q].reshape(rows, width) for q in range(per_owner)], axis=0)
    scores = dot(query, new, NT) * scale
    half = OWN_TOK // 2
    column = iota(scores.shape, 1)
    core = jnp.where(column < scores.shape[1] // 2, rank_ref[0] % 2, 1 - rank_ref[0] % 2)
    place = core * half + column % half
    owner_row = iota(scores.shape, 0) // rows
    first = jnp.zeros(scores.shape, i32)
    last = jnp.zeros(scores.shape, i32)
    start = jnp.int32(0)
    for q in range(per_owner):
        end = start + len_ref[q]
        first = jnp.where(owner_row == q, start, first)
        last = jnp.where(owner_row == q, end, last)
        start = end
    scores = jnp.where((place >= first) & (place < last), scores, masked_score)
    total_rows = per_owner * rows
    side = side_ref[...].reshape(total_rows, 128)
    old_top, old_sum = side[:, :1], side[:, 1:2]
    top = jnp.maximum(jnp.max(scores, axis=1, keepdims=True), old_top)
    scores = jnp.exp(scores - top)
    weight = jnp.exp(old_top - top)
    total = jnp.sum(scores, axis=1, keepdims=True) + old_sum * weight
    acc = acc_ref[...].reshape(total_rows, LAT) * weight + dot(scores.astype(bf16), new[:, :LAT])
    latent = (acc / total).astype(bf16)
    values = uv_ref.shape[2]
    groups = per_owner * steps
    each = out_ref.shape[3] // values
    for h in range(0, heads, 2):
        full = dot(latent, jnp.concatenate([uv_ref[h], uv_ref[h + 1]], axis=1))
        full = full.reshape(groups, heads, 2 * values)
        wanted = h + iota(full.shape, 2) // values
        mine = jnp.sum(jnp.where(iota(full.shape, 1) == wanted, full, 0.0), axis=1).astype(bf16)
        place = (h % each) * values
        out_ref[:, h // each, :, place : place + 2 * values] = jnp.broadcast_to(
            mine[None], (out_ref.shape[0], groups, 2 * values)
        )


def attend_new(rank, my_lengths, queries, new_rows, other_rows, acc, side, w_uv, dp, parts):
    steps, per_owner, heads, _ = queries.shape
    whole = pl.BlockSpec(memory_space=pltpu.VMEM)
    return call(
        merge_kernel,
        jax.ShapeDtypeStruct(
            (dp // parts, parts, per_owner * steps, heads // parts * w_uv.shape[2]), bf16
        ),
        (8 * new_rows.size * per_owner * steps * heads, 2 * w_uv.size),
        grid=(1,),
        in_specs=[
            pl.BlockSpec(memory_space=pltpu.SMEM),
            pl.BlockSpec(memory_space=pltpu.SMEM),
            whole,
            whole,
            whole,
            pl.BlockSpec(acc.shape, lambda c: (0, 0, 0)),
            pl.BlockSpec(side.shape, lambda c: (0, 0, 0)),
            whole,
        ],
        out_specs=whole,
        name="attend_new",
    )(rank, my_lengths, queries, new_rows, other_rows, in_hbm(acc), in_hbm(side), w_uv)


def own_heads_kernel(rank_ref, w_ref, out_ref):
    heads, _, values = w_ref.shape
    for h in range(heads):
        out_ref[:, h * values : (h + 1) * values] = w_ref[h]


def own_heads(rank, own, ring):
    total, features, values = own.shape
    heads = total // ring
    return call(
        own_heads_kernel,
        jax.ShapeDtypeStruct((features, heads * values), bf16),
        (0, 4 * heads * features * values),
        grid_spec=pltpu.PrefetchScalarGridSpec(
            num_scalar_prefetch=1,
            grid=(1,),
            in_specs=[pl.BlockSpec((heads, features, values), lambda c, rank: (rank[0], 0, 0))],
            out_specs=pl.BlockSpec(memory_space=pltpu.VMEM),
        ),
        name="own_heads",
    )(rank, in_hbm(own))


def project_kernel(rank_ref, x_ref, own_ref, *refs):
    *w_refs, out_ref = refs
    ring, tp = out_ref.shape[:2]
    x = x_ref[...].T
    for k in range(ring):
        if k == 0:
            weights = own_ref[...]
        else:
            w_ref = w_refs[k - 1]
            weights = jnp.concatenate([w_ref[h] for h in range(w_ref.shape[0])], axis=1)
        width = weights.shape[0] // tp
        target = (rank_ref[0] + ring - k) % ring
        value = dot(weights, x)
        spare = jnp.zeros((PAD - width, value.shape[1]), f32)
        for j in range(tp):
            part = jnp.concatenate([value[j * width : (j + 1) * width], spare], axis=0)
            out_ref[target, j] = part.astype(bf16)


def project(rank, own, pieces, every, tp):
    ring, columns = 1 + len(pieces), every.shape[0]
    whole = pl.BlockSpec(memory_space=pltpu.VMEM)
    return call(
        project_kernel,
        jax.ShapeDtypeStruct((ring, tp, PAD, columns), bf16),
        (2 * ring * own.size * columns, 2 * (ring * own.size + every.size)),
        in_specs=[pl.BlockSpec(memory_space=pltpu.SMEM)] + [whole] * (1 + ring),
        out_specs=whole,
        name="project",
    )(rank, every, own, *pieces)


def split_sum(value):
    high = value.astype(bf16).astype(f32)
    return high, value - high


def stack_halves(value, width):
    half = value.shape[1] // 2
    return jnp.concatenate([value[:width, :half], value[:width, half:]], axis=0)


def mixed_kernel(width, part_ref, hidden_ref, mixed_ref, out_ref):
    mixed = jnp.sum(part_ref[...].astype(f32), axis=0) + hidden_ref[...]
    mixed_ref[...] = mixed
    sent = stack_halves(mixed, width).astype(bf16)
    out_ref[...] = jnp.broadcast_to(sent[None], out_ref.shape)


def make_mixed(parts, hidden_t, dp, width):
    _, rows, columns = parts.shape
    return call(
        functools.partial(mixed_kernel, width),
        (
            jax.ShapeDtypeStruct((rows, columns), f32),
            jax.ShapeDtypeStruct((dp, 2 * width, columns // 2), bf16),
        ),
        (parts.size, 4 * parts.size),
        name="make_mixed",
    )(parts, hidden_t)


def gate_kernel(groups, rank_ref, x_ref, *refs):
    *w_refs, keep_ref, send_ref = refs
    units = w_refs[0].shape[1]
    width = x_ref.shape[1] // 2
    blocks = []
    for c in range(0, x_ref.shape[0], GROUP):
        for slot in range(GROUP):
            piece = x_ref[c + source_in_group(rank_ref[0], slot)].astype(f32)
            spare = jnp.zeros((PAD - width, piece.shape[1]), f32)
            right = jnp.concatenate([piece[width:], spare], axis=0)
            blocks.append(jnp.concatenate([piece[:PAD], right], axis=1))
    x = jnp.concatenate(blocks, axis=0)
    squares = jnp.where(iota(x.shape, 0) % PAD < width, x * x, 0.0)
    high, low = split_sum(jnp.sum(squares, axis=0, keepdims=True))
    row = iota((16, x.shape[1]), 0)
    tail = jnp.where(row == 0, high, jnp.where(row == 1, low, 0.0)).astype(bf16)
    x = x.astype(bf16)
    for w_ref, group in zip(w_refs, groups):
        for at, k in enumerate(group):
            n = partner(rank_ref[0], 2 * keep_ref.shape[0], k, -1) // 2
            out_ref = send_ref if k % 2 else keep_ref
            out_ref[n, :units, :] = dot(w_ref[at], x).astype(bf16)
            out_ref[n, units:, :] = tail


def collect_kernel(*refs):
    for n, w_ref in enumerate(refs[:-1]):
        lanes = w_ref.shape[3]
        for c in range(w_ref.shape[1]):
            refs[-1][n, :, c * lanes : (c + 1) * lanes] = w_ref[0, c]


def collect(pieces, places, units):
    tp = len(pieces)
    _, count, _, lanes = pieces[0][0].shape
    out_shape = (tp, units, count * lanes)
    return call(
        collect_kernel,
        jax.ShapeDtypeStruct(out_shape, bf16),
        (0, 4 * tp * units * count * lanes),
        grid=(1,),
        in_specs=[
            pl.BlockSpec((1, count, units, lanes), lambda c, at=at: (at, 0, 0, 0)) for _, at in pieces
        ],
        out_specs=pl.BlockSpec(memory_space=pltpu.VMEM),
        name="collect",
    )(*[place(array) for (array, _), place in zip(pieces, places)])


def gate_up(rank, weights, groups, x):
    tp = sum(len(group) for group in groups)
    _, units, depth = weights[0].shape
    size = tp * units * depth
    columns = 2 * x.shape[2]
    whole = pl.BlockSpec(memory_space=pltpu.VMEM)
    out = jax.ShapeDtypeStruct((tp // 2, units + 16, columns), bf16)
    return call(
        functools.partial(gate_kernel, groups),
        (out, out),
        (2 * size * columns, 2 * size + 2 * x.size),
        in_specs=[pl.BlockSpec(memory_space=pltpu.SMEM)] + [whole] * (1 + len(weights)),
        out_specs=(whole, whole),
        name="gate_up",
    )(rank, x, *weights)


def add_kernel(units, a_ref, b_ref, out_ref):
    out_ref[:, :units, :] = (
        a_ref[:, :units, :].astype(f32) + b_ref[:, :units, :].astype(f32)
    ).astype(bf16)
    tail = a_ref[:, units:, :].astype(f32) + b_ref[:, units:, :].astype(f32)
    high, low = split_sum(tail[:, 0:1] + tail[:, 1:2])
    row = iota(tail.shape, 1)
    tail = jnp.where(row == 0, high, jnp.where(row == 1, low, 0.0))
    out_ref[:, units:, :] = tail.astype(bf16)


def add_cores(a, b, units):
    return call(
        functools.partial(add_kernel, units),
        jax.ShapeDtypeStruct(a.shape, bf16),
        (2 * a.size, 6 * a.size),
        name="add_cores",
    )(a, b)


def activate_kernel(model_width, units, part_ref, out_ref):
    sums = jnp.sum(part_ref[...].astype(f32), axis=0)
    squares = sums[2 * units : 2 * units + 1] + sums[2 * units + 1 : 2 * units + 2]
    factor = lax.rsqrt(squares / model_width + norm_eps)
    gate = sums[:units] * factor
    up = sums[units : 2 * units] * factor
    value = gate / (1.0 + jnp.exp(-gate)) * up
    spare = out_ref.shape[1] - units
    if spare:
        value = jnp.concatenate([value, jnp.zeros((spare, value.shape[1]), f32)], axis=0)
    out_ref[...] = jnp.broadcast_to(value.astype(bf16)[None], out_ref.shape)


def activate(parts, model_width, units, unit_pad):
    tp, _, columns = parts.shape
    return call(
        functools.partial(activate_kernel, model_width, units),
        jax.ShapeDtypeStruct((tp, unit_pad, columns), bf16),
        (10 * parts.size, 4 * parts.size),
        name="activate",
    )(parts)


def down_kernel(rank_ref, w_ref, same_ref, other_ref, out_ref):
    tp = 2 * same_ref.shape[0]
    refs = (same_ref, other_ref)
    sources = [partner(rank_ref[0], tp, k, -1) // 2 for k in range(tp)]
    x = jnp.concatenate([refs[k % 2][n] for k, n in enumerate(sources)], axis=0)
    value = dot(w_ref[...], x)
    count, rows, _ = out_ref.shape
    value = value.reshape(count, PAD, value.shape[1])
    for n in range(count):
        first, slot = n // GROUP * GROUP, n % GROUP
        out_ref[first + source_in_group(rank_ref[0], slot)] = stack_halves(
            value[n], rows // 2
        ).astype(bf16)


def down(rank, turned, same, other, dp, width):
    rows, depth = turned.shape
    columns = same.shape[2]
    block = 256 if rows % 256 == 0 else 128
    x_spec = pl.BlockSpec(same.shape, lambda c: (0, 0, 0))
    return call(
        down_kernel,
        jax.ShapeDtypeStruct((dp, 2 * width, columns // 2), bf16),
        (2 * turned.size * columns, 2 * turned.size + 4 * same.size),
        grid=(rows // block,),
        in_specs=[
            pl.BlockSpec(memory_space=pltpu.SMEM),
            pl.BlockSpec((block, depth), lambda c: (c, 0)),
            x_spec,
            x_spec,
        ],
        out_specs=pl.BlockSpec((block // PAD, 2 * width, columns // 2), lambda c: (c, 0, 0)),
        name="down",
    )(rank, turned, same, other)


def finish_kernel(dp, per_owner, steps, part_ref, mixed_ref, out_ref):
    value = jnp.sum(part_ref[...].astype(f32), axis=0)
    width = value.shape[0] // 2
    value = jnp.concatenate([value[:width], value[width:]], axis=1) + mixed_ref[:width]
    picked = dot(value.astype(bf16), token_picker(dp, per_owner, steps), NT)
    picked = picked.astype(bf16)
    each = out_ref.shape[2]
    for s in range(steps):
        out_ref[:, s, :] = picked[:, s * each : (s + 1) * each]


def exchange(x, axis, groups=None):
    return lax.all_to_all(
        x, axis, split_axis=0, concat_axis=0, tiled=True, axis_index_groups=groups
    )


def swap_cores(x):
    return lax.ppermute(x, "tp", [(j, j ^ 1) for j in range(lax.axis_size("tp"))])


def shards(
    prefill_latent,
    request_slot,
    new_lengths,
    ctx_lengths,
    kv_cache,
    queries,
    step_latents,
    w_uv,
    w_out,
    hidden,
    ffn_gain,
    w_gate,
    w_up,
    w_down,
):
    both = ("z", "y")
    ring = lax.axis_size("y")
    dp, tp = lax.axis_size("z") * ring, lax.axis_size("tp")
    dp_rank, tp_rank = lax.axis_index(both), lax.axis_index("tp")
    steps, per_owner = queries.shape[:2]
    width = hidden.shape[2]
    model_width = width * dp * tp
    units = w_gate.shape[1]
    unit_pad = -(-units // 16) * 16
    total = hidden.shape[0] * hidden.shape[1]

    rank = tp_rank.astype(i32).reshape(1)
    routed = route(rank, request_slot, new_lengths, prefill_latent)
    incoming = exchange(routed.reshape(dp, OWN_TOK // 2, -1), both).reshape(routed.shape)

    arrays = reshard(rank, ffn_gain, w_gate, w_up, w_down, dp, tp, width, unit_pad)

    y_rank = lax.axis_index("y").astype(i32).reshape(1)
    each = w_out.shape[0] // ring
    w_turned = w_out.transpose(0, 2, 1)
    out_pieces = [
        lax.dynamic_slice_in_dim(w_turned, (y_rank[0] + k) % ring * each, each, 0)
        for k in range(1, ring)
    ]
    incoming, _ = lax.optimization_barrier((incoming, out_pieces))
    out_pieces = [
        lax.ppermute(piece, "y", [(j, (j + k) % ring) for j in range(ring)])
        for k, piece in enumerate(out_pieces, 1)
    ]

    ctx_lengths, _ = lax.optimization_barrier((ctx_lengths, arrays[0]))
    tokens = jnp.pad(step_latents.transpose(1, 0, 2), ((0, 0), (0, 16 - steps), (0, 0)))
    acc, side = attend_cache(
        ctx_lengths, queries, in_hbm(kv_cache.transpose(0, 2, 1)), tokens
    )
    my_lengths = lax.dynamic_index_in_dim(new_lengths, dp_rank, 0, keepdims=False)
    heads_out = attend_new(
        rank, my_lengths, queries, incoming, swap_cores(incoming), acc, side, w_uv, dp, ring
    )
    every = exchange(heads_out.reshape((dp,) + heads_out.shape[2:]), both).reshape(total, -1)

    def along_x(piece, k, sign):
        return lax.ppermute(piece, "tp", [(j, partner(j, tp, k, sign)) for j in range(tp)])

    pieces = {k: (arrays[n], at) for k, (n, at) in piece_places(tp).items()}
    if tp > 2:
        plus, minus = along_x(arrays[2], 2, 1), along_x(arrays[3], 2, -1)
        far, _ = lax.optimization_barrier((arrays[4:6], (plus, minus)))
        far = [along_x(far[0], 2, 1), along_x(far[1], 2, -1)]
        every, _ = lax.optimization_barrier((every, (plus, minus, far)))
    parts = project(y_rank, own_heads(y_rank, w_turned, ring), out_pieces, every, tp)
    parts = exchange(parts.reshape((ring * tp,) + parts.shape[2:]), ("y", "tp"))
    if tp > 2:
        pieces[2], pieces[6] = (plus, 0), (minus, 0)
        swapped = [along_x(plus[1:], 1, 1), along_x(minus[1:], 1, 1)]
        far = [along_x(far[0], 2, 1), along_x(far[1], 3, -1)]
        parts, _ = lax.optimization_barrier((parts, far))
        pieces[3], pieces[7] = (swapped[0], 0), (swapped[1], 0)
        pieces[4], pieces[5] = (far[0], 0), (far[1], 0)
    pieces[1] = along_x(arrays[1], 1, 1), 0
    pieces = [pieces[k] for k in range(tp)]
    hidden_t = call(
        functools.partial(hidden_kernel, dp, per_owner, steps),
        jax.ShapeDtypeStruct((PAD, total), f32),
        name="turn_hidden",
    )(hidden.transpose(2, 0, 1).reshape(width, total))
    mixed, sent = make_mixed(parts, hidden_t, dp, width)
    x = exchange(sent, both)
    groups = [[k for k in range(tp) if k // 2 != 2], [k for k in range(tp) if k // 2 == 2]]
    groups = [group for group in groups if group]
    places = [(lambda array: array) if k // 2 == 2 else in_hbm for k in range(tp)]
    weights = [
        collect([pieces[k] for k in group], [places[k] for k in group], 2 * units)
        for group in groups
    ]
    keep, send = gate_up(rank, weights, groups, x)
    along = [[2 * n + core for n in range(tp // 2)] for core in range(2)]
    parts = exchange(add_cores(keep, swap_cores(send), 2 * units), "tp", along)
    parts, turned_down = lax.optimization_barrier((parts, turn(pieces, [in_hbm] * tp, 2 * units)))
    same = exchange(activate(parts, model_width, units, unit_pad), "tp", along)
    other = swap_cores(same)
    parts = exchange(down(rank, turned_down, same, other, dp, width), both)
    out = call(
        functools.partial(finish_kernel, dp, per_owner, steps),
        jax.ShapeDtypeStruct((width, steps, total // steps), bf16),
        name="finish",
    )(parts, mixed)
    return out.transpose(1, 2, 0)


def solution(mesh):
    devices = mesh.devices
    ring = 2
    devices = devices.reshape(devices.shape[0] // ring, ring, devices.shape[1])
    dp, tp = ("z", "y"), "tp"
    every = ("z", "y", "tp")
    return jax.shard_map(
        shards,
        mesh=jax.sharding.Mesh(devices, every),
        in_specs=(
            P(dp, None),
            P(),
            P(),
            P(dp),
            P(dp, None, None),
            P(None, dp, tp, None),
            P(None, dp, None),
            P(tp, None, None),
            P(tp, None, dp),
            P(None, None, every),
            P(),
            P(None, every),
            P(None, every),
            P(every, None),
        ),
        out_specs=P(None, None, every),
        check_vma=False,
    )
```
